1024 devices in a mesh: fsdp: 256 (over z, x_lo, y), tp: 4 (over x_hi, core).
Axes of the slice: x: 4 (x_hi: 2, x_lo: 2; x = x_hi * 2 + x_lo), y: 8, z: 16, core: 2. Of those that a mesh axis runs over, the one named last changes fastest.
Arguments:
- inputs: bfloat16 [65536, 4096], P('fsdp'), may hold values from -24 to 24
- value_grad: bfloat16 [65536, 1024], P('fsdp', 'tp'), may hold values from -24 to 24
- value_weight: bfloat16 [4096, 1024], P('tp', 'fsdp'), may hold values from -0.09375 to 0.09375
- counts: int32 [256, 4], P('fsdp'), may hold values from 1 to 232, as said below
- offsets: int32 [256, 4], P('fsdp'), may hold values from 0 to 248, as said below
Outputs:
- input_grad: bfloat16 [65536, 4096], P('fsdp', 'tp')
- weight_grad: float32 [4096, 1024], P('fsdp', 'tp')
The draws below stay inside these ranges and needn't reach their ends.
Inputs may be any that keep to these rules, and one draw needn't show every extreme that they name: `offsets`: on each index of fsdp the 4 samples lie in order; each starts at a multiple of 8, at or after the 8-row-aligned end of the previous one, and all lie within the 256 rows; on some index the aligned blocks of its samples fill all 256 rows. `counts`: how many rows the samples of a row group fill varies widely between indices of fsdp.
All inputs are finite; a program needn't handle non-finite values.
Results may differ from the reference program's by a relative error of at most 0.0046.
Values may be sent and summed in bfloat16 or wider, within the bound.
No kernel may reach another device: no remote copies, remote signals or barrier semaphores. Data moves between devices by JAX's collectives and lax.ppermute only.
A program may use at most 32 MiB of HBM per device.

```python
import math
import jax
import jax.numpy as jnp
from jax import lax

D = 4096
KV = 1024
TOK_DEV = 256
S_DEV = 4
TOKENS = 65536
SAMPLES = 1024
N_FSDP = 256


def packing_layout(key):
    units_all = TOK_DEV // 8
    spare = units_all - S_DEV
    divisor = max(spare, 1)
    first = jax.random.randint(jax.random.fold_in(key, 101), (N_FSDP,), 0, spare + 1)
    second = jax.random.randint(jax.random.fold_in(key, 102), (N_FSDP,), 0, spare + 1)
    extra = first * second // divisor
    chosen = jax.random.randint(jax.random.fold_in(key, 103), (), 0, N_FSDP)
    is_chosen = jnp.arange(N_FSDP) == chosen
    extra = jnp.where(is_chosen, spare, extra)
    raw_cuts = jax.random.randint(jax.random.fold_in(key, 104), (N_FSDP, S_DEV - 1), 0, spare + 1)
    cuts = jnp.sort(raw_cuts * extra[:, None] // divisor, axis=1)
    cuts = jnp.where(is_chosen[:, None], spare, cuts)
    edges = jnp.concatenate([jnp.zeros((N_FSDP, 1), jnp.int32), cuts.astype(jnp.int32), extra[:, None].astype(jnp.int32)], axis=1)
    units = 1 + edges[:, 1:] - edges[:, :-1]
    ends = jnp.cumsum(units, axis=1)
    offsets = (8 * (ends - units)).astype(jnp.int32)
    trims = jax.random.randint(jax.random.fold_in(key, 105), (N_FSDP, S_DEV), 0, 8)
    slots = jnp.arange(S_DEV)[None, :]
    fixed_trims = jnp.where(slots == S_DEV - 1, 7, 0)
    trims = jnp.where(is_chosen[:, None], fixed_trims, trims)
    counts = (8 * units - trims).astype(jnp.int32)
    return (counts, offsets)


def draw_counts(key, part):
    return packing_layout(key)[0]


def draw_offsets(key, part):
    return packing_layout(key)[1]


def strengthened(result, own_key, source, target, shards_of, factor):
    def block_of(dim):
        return (jnp.arange(result.shape[dim]) // (result.shape[dim] // shards_of)).reshape((-1,) + (1,) * (result.ndim - 1 - dim))

    near = jax.random.permutation(own_key, shards_of)[block_of(target)]
    second = (block_of(target) + shards_of // 2) % shards_of
    return jnp.where((block_of(source) == near) | (block_of(source) == second), factor * result, result)


def block_scale(key, extent, cuts, low, high):
    factor_of = 1.0
    for position, parts in cuts:
        heights = jax.random.uniform(jax.random.fold_in(jax.random.fold_in(key, 6), position), (parts,), jnp.float32, low / len(cuts), high / len(cuts))
        factor_of = factor_of * jnp.repeat(jnp.exp(heights), extent[position] // parts).reshape((-1,) + (1,) * (len(extent) - 1 - position))
    return factor_of


def gaussian(stream_key, shape, width, most, pieces=(), kind=jnp.bfloat16):
    level = block_scale(stream_key, shape, pieces, -0.22, 0.18) if pieces else 1.0
    entries = jax.random.normal(stream_key, shape, jnp.float32) * width * level
    return jnp.minimum(jnp.maximum(entries, -most), most).astype(kind)


def heavy_noise(stream_key, shape, deviation, limit, cuts, heavy, kind=jnp.bfloat16):
    result = deviation * jax.random.normal(stream_key, shape, jnp.float32)
    if cuts:
        result = result * block_scale(stream_key, shape, cuts, -0.22, 0.18)
    return jnp.clip(strengthened(result, jax.random.fold_in(stream_key, 3), *heavy), -limit, limit).astype(kind)


def setup_inputs(seed: int = 0) -> dict:
    keys = jax.random.split(jax.random.key(seed), 6)
    inputs = heavy_noise(keys[0], (TOKENS, D), 1.0, 24.0, ((0, 256),), (0, 1, 256, 6.0))
    value_grad = gaussian(keys[1], (TOKENS, KV), 4.0, 24.0, ((0, 256), (1, 4)))
    value_weight = gaussian(keys[2], (D, KV), D ** -0.5, 0.09375, ((0, 4), (1, 256)))
    counts = draw_counts(jax.random.fold_in(keys[5], 71), 0)
    offsets = draw_offsets(jax.random.fold_in(keys[5], 71), 0)
    return {"inputs": inputs, "value_grad": value_grad, "value_weight": value_weight, "counts": counts, "offsets": offsets}


def reference(inputs, value_grad, value_weight, counts, offsets):
    positions = jnp.arange(TOK_DEV, dtype=jnp.int32)[None, :, None]
    inside = (positions >= offsets[:, None, :]) & (positions < offsets[:, None, :] + counts[:, None, :])
    inverse_root = lax.rsqrt(counts.astype(jnp.float32))[:, None, :]
    row_factor = lax.optimization_barrier(jnp.sum(jnp.where(inside, inverse_root, jnp.zeros_like(inverse_root)), axis=2))
    scaled = (value_grad.astype(jnp.float32).reshape(N_FSDP, TOK_DEV, KV) * row_factor[:, :, None]).astype(jnp.bfloat16)

    def rows_grad(group_rows):
        return jnp.dot(group_rows, value_weight.T, preferred_element_type=jnp.float32).astype(jnp.bfloat16)
    input_grad = lax.map(rows_grad, scaled).reshape(TOKENS, D)
    weight_grad = jnp.dot(inputs.T, scaled.reshape(TOKENS, KV), preferred_element_type=jnp.float32)
    weight_grad = weight_grad * (1.0 / math.sqrt(SAMPLES))
    return (input_grad, weight_grad)
```

```python
import math

import jax
import jax.numpy as jnp
from jax import lax
from jax.experimental import pallas as pl
from jax.experimental.pallas import tpu as pltpu
from jax.sharding import Mesh
from jax.sharding import PartitionSpec as P

FSDP = ("z", "xl", "y")
TP = ("xh", "c")
VMEM_LIMIT = 48 * 1024 * 1024


def prep_kernel(place_ref, counts_ref, offsets_ref, grad_ref, inputs_ref, scaled_ref, send_ref, sems):
    half = place_ref[0]
    blocks = send_ref.shape[1] // 128
    copies = []
    for z in range(blocks):
        source = pl.ds(pl.multiple_of((2 * z + 1 - half) * 128, 128), 128)
        copy = pltpu.make_async_copy(
            inputs_ref.at[:, source], send_ref.at[:, pl.ds(z * 128, 128)], sems.at[z]
        )
        copy.start()
        copies.append(copy)
    rows, columns = grad_ref.shape
    positions = lax.broadcasted_iota(jnp.int32, (rows, columns), 0)
    length = jnp.zeros((rows, columns), jnp.int32)
    for s in range(counts_ref.shape[1]):
        first = offsets_ref[0, s]
        count = counts_ref[0, s]
        length = jnp.where((positions >= first) & (positions < first + count), count, length)
    factor = jnp.where(length > 0, lax.rsqrt(jnp.maximum(length, 1).astype(jnp.float32)), 0.0)
    scaled_ref[...] = (grad_ref[...].astype(jnp.float32) * factor).astype(jnp.bfloat16)
    for copy in copies:
        copy.wait()


def weight_kernel(place_ref, inputs_ref, received_ref, own_ref, all_ref, out_ref):
    half = place_ref[0]
    peer = all_ref[place_ref[1]]
    own = own_ref[...]
    peers = out_ref.shape[0]
    for z in range(received_ref.shape[1] // 128):
        mine = inputs_ref[:, pl.ds(pl.multiple_of((2 * z + half) * 128, 128), 128)]
        other = received_ref[:, z * 128 : (z + 1) * 128]
        dims = (((0,), (0,)), ((), ()))
        term = lax.dot_general(mine, own, dims, preferred_element_type=jnp.float32)
        term += lax.dot_general(other, peer, dims, preferred_element_type=jnp.float32)
        each = 128 // peers
        out_ref[:, z * each : (z + 1) * each, :] = term.reshape(peers, each, -1).astype(jnp.bfloat16)


def input_kernel(all_ref, weight_ref, out_ref):
    groups = out_ref.shape[0]
    parts = all_ref.shape[0] // groups
    wide = all_ref.shape[2]
    for g in range(groups):
        total = None
        for t in range(parts):
            term = jnp.dot(
                all_ref[g * parts + t],
                weight_ref[t * wide : (t + 1) * wide, :],
                preferred_element_type=jnp.float32,
            )
            total = term if total is None else total + term
        out_ref[g] = total.astype(jnp.bfloat16)


def in_vmem():
    return pl.BlockSpec(memory_space=pltpu.VMEM)


def in_smem():
    return pl.BlockSpec(memory_space=pltpu.SMEM)


def anywhere():
    return pl.BlockSpec(memory_space=pl.ANY)


PARAMS = pltpu.CompilerParams(vmem_limit_bytes=VMEM_LIMIT)


def local(inputs, value_grad, value_weight, counts, offsets):
    rows, features = inputs.shape
    columns = value_grad.shape[1]
    quarter, own_columns = value_weight.shape
    half = lax.axis_index("xl")
    tensor = lax.axis_index(TP)
    n_tp = lax.axis_size(TP)
    n_z = lax.axis_size("z")
    n_y = lax.axis_size("y")

    mine = value_weight.T.reshape(own_columns, 2, quarter // 2).transpose(1, 0, 2)
    mine = jnp.broadcast_to(mine[:, None], (2, n_y, own_columns, quarter // 2))
    mine = mine.reshape(2 * n_y, own_columns, quarter // 2)
    block = lax.all_to_all(mine, ("xl", "y"), 0, 0, tiled=True)
    block = block.reshape(2 * n_y * own_columns, quarter // 2)
    weight = lax.all_gather(block, "z", axis=0, tiled=True)

    place = jnp.stack([half, (1 - half) * n_tp + tensor]).astype(jnp.int32)
    scaled, send = pl.pallas_call(
        prep_kernel,
        out_shape=(
            jax.ShapeDtypeStruct((rows, columns), jnp.bfloat16),
            jax.ShapeDtypeStruct((rows, features // 2), jnp.bfloat16),
        ),
        in_specs=[in_smem(), in_smem(), in_smem(), in_vmem(), anywhere()],
        out_specs=(in_vmem(), anywhere()),
        scratch_shapes=[pltpu.SemaphoreType.DMA((features // 256,))],
        compiler_params=PARAMS,
    )(place, counts, offsets, value_grad, inputs)

    received = lax.ppermute(send, "xl", [(0, 1), (1, 0)])
    copies = jnp.broadcast_to(scaled, (2 * n_tp, rows, columns))
    scaled_all = lax.all_to_all(copies, ("xl", *TP), 0, 0, tiled=True)

    term = pl.pallas_call(
        weight_kernel,
        out_shape=jax.ShapeDtypeStruct((n_y, features // 2 // n_y, columns), jnp.bfloat16),
        in_specs=[in_smem(), in_vmem(), in_vmem(), in_vmem(), in_vmem()],
        out_specs=in_vmem(),
        compiler_params=PARAMS,
    )(place, inputs, received, scaled, scaled_all)
    terms = lax.all_to_all(term, "y", 0, 0, tiled=True)
    summed = jnp.sum(terms.astype(jnp.float32), axis=0)
    summed = summed.reshape(n_z, -1, columns)
    summed = lax.all_to_all(summed, "z", 0, 0, tiled=True)
    normalizer = 1.0 / math.sqrt(counts.shape[1] * lax.axis_size(FSDP))
    weight_grad = jnp.sum(summed, axis=0) * normalizer

    halves = pl.pallas_call(
        input_kernel,
        out_shape=jax.ShapeDtypeStruct((2, rows, quarter // 2), jnp.bfloat16),
        in_specs=[in_vmem(), in_vmem()],
        out_specs=in_vmem(),
        compiler_params=PARAMS,
    )(scaled_all, weight)
    halves = lax.all_to_all(halves, "xl", 0, 0, tiled=True)
    input_grad = jnp.concatenate([halves[0], halves[1]], axis=1)
    return (input_grad, weight_grad)


def solution(mesh):
    split = Mesh(mesh.devices.reshape(16, 2, 8, 2, 2), (*FSDP, *TP))
    in_specs = (P(FSDP, None), P(FSDP, TP), P(TP, FSDP), P(FSDP, None), P(FSDP, None))
    out_specs = (P(FSDP, TP), P(FSDP, TP))
    return jax.shard_map(local, mesh=split, in_specs=in_specs, out_specs=out_specs, check_vma=False)
```

```python
import functools
import math

import jax
import jax.numpy as jnp
from jax import lax
from jax.experimental import pallas as pl
from jax.experimental.pallas import tpu as pltpu
from jax.sharding import Mesh
from jax.sharding import PartitionSpec as P

FSDP = ("z", "xl", "y")
TP = ("xh", "c")
SWAP = [(0, 1), (1, 0)]
VMEM_LIMIT = 24 * 1024 * 1024
PREP_LIMIT = 60 * 1024 * 1024


def prep_kernel(place_ref, counts_ref, offsets_ref, grad_ref, inputs_ref, scaled_ref, send_ref, sems):
    half = place_ref[0]
    rows, columns = grad_ref.shape
    wide = send_ref.shape[1] - columns
    blocks = wide // 128
    copies = []
    for z in range(blocks):
        source = pl.ds(pl.multiple_of((2 * z + 1 - half) * 128, 128), 128)
        copies.append(
            pltpu.make_async_copy(
                inputs_ref.at[:, source], send_ref.at[:, pl.ds(z * 128, 128)], sems.at[z]
            )
        )
        copies[-1].start()
    positions = lax.broadcasted_iota(jnp.int32, (rows, columns), 0)
    length = jnp.zeros((rows, columns), jnp.int32)
    for s in range(counts_ref.shape[1]):
        first = offsets_ref[0, s]
        count = counts_ref[0, s]
        length = jnp.where((positions >= first) & (positions < first + count), count, length)
    factor = jnp.where(length > 0, lax.rsqrt(jnp.maximum(length, 1).astype(jnp.float32)), 0.0)
    scaled_ref[...] = (grad_ref[...].astype(jnp.float32) * factor).astype(jnp.bfloat16)
    copies.append(
        pltpu.make_async_copy(scaled_ref, send_ref.at[:, pl.ds(wide, columns)], sems.at[blocks])
    )
    copies[-1].start()
    for copy in copies:
        copy.wait()


def weight_kernel(place_ref, inputs_ref, received_ref, own_ref, out_ref):
    half = place_ref[0]
    own = own_ref[...]
    wide = received_ref.shape[1] - own.shape[1]
    peer = received_ref[:, wide:]
    peers = out_ref.shape[0]
    for z in range(wide // 128):
        mine = inputs_ref[:, pl.ds(pl.multiple_of((2 * z + half) * 128, 128), 128)]
        other = received_ref[:, z * 128 : (z + 1) * 128]
        dims = (((0,), (0,)), ((), ()))
        term = lax.dot_general(mine, own, dims, preferred_element_type=jnp.float32)
        term += lax.dot_general(other, peer, dims, preferred_element_type=jnp.float32)
        each = 128 // peers
        out_ref[:, z * each : (z + 1) * each, :] = term.reshape(peers, each, -1).astype(jnp.bfloat16)


def order_kernel(sizes, place_ref, own_ref, core_ref, far_ref, both_ref, out_ref):
    tensor = place_ref[1]
    parts = [own_ref, core_ref, far_ref, both_ref]
    wide = own_ref.shape[1]
    n_z, n_y, n_j = sizes
    total = len(parts) * wide
    spot = lax.broadcasted_iota(jnp.int32, (1, total), 1)
    j = spot % n_j
    z = (spot // n_j) % n_z
    xl = (spot // (n_j * n_z)) % 2
    y = spot // (n_j * n_z * 2)
    source = ((z * 2 + xl) * n_y + y) * n_j + j
    for c in range(0, total, 256):
        moved = None
        for p, part in enumerate(parts):
            row = lax.broadcasted_iota(jnp.int32, (wide, 256), 0) + (tensor ^ p) * wide
            pick = (row == source[:, c : c + 256]).astype(jnp.float32).astype(jnp.bfloat16)
            term = jnp.dot(part[...], pick, preferred_element_type=jnp.float32)
            moved = term if moved is None else moved + term
        out_ref[:, c : c + 256] = moved.astype(jnp.bfloat16)


def input_kernel(scaled_ref, weight_ref, own_ref, peer_ref):
    rows = own_ref.shape[0]
    for g, out_ref in enumerate((own_ref, peer_ref)):
        out_ref[...] = jnp.dot(
            scaled_ref[g * rows : (g + 1) * rows, :],
            weight_ref[...],
            preferred_element_type=jnp.float32,
        ).astype(jnp.bfloat16)


def in_vmem():
    return pl.BlockSpec(memory_space=pltpu.VMEM)


def in_smem():
    return pl.BlockSpec(memory_space=pltpu.SMEM)


def anywhere():
    return pl.BlockSpec(memory_space=pl.ANY)


PARAMS = pltpu.CompilerParams(vmem_limit_bytes=VMEM_LIMIT)


def local(inputs, value_grad, value_weight, counts, offsets):
    rows, features = inputs.shape
    columns = value_grad.shape[1]
    quarter, own_columns = value_weight.shape
    half = lax.axis_index("xl")
    n_tp = lax.axis_size(TP)
    n_z = lax.axis_size("z")
    n_y = lax.axis_size("y")
    wide = features // 2

    place = jnp.stack([half, lax.axis_index(TP)]).astype(jnp.int32)
    scaled, send = pl.pallas_call(
        prep_kernel,
        out_shape=(
            jax.ShapeDtypeStruct((rows, columns), jnp.bfloat16),
            jax.ShapeDtypeStruct((rows, wide + columns), jnp.bfloat16),
        ),
        in_specs=[in_smem(), in_smem(), in_smem(), in_vmem(), anywhere()],
        out_specs=(in_vmem(), anywhere()),
        scratch_shapes=[pltpu.SemaphoreType.DMA((wide // 128 + 1,))],
        compiler_params=pltpu.CompilerParams(vmem_limit_bytes=PREP_LIMIT),
    )(place, counts, offsets, value_grad, inputs)
    send, value_weight = lax.optimization_barrier((send, value_weight))
    received = lax.ppermute(send, "xl", SWAP)

    mine = value_weight.T.reshape(own_columns, 2, quarter // 2).transpose(1, 0, 2)
    mine = jnp.broadcast_to(mine[:, None], (2, n_z, own_columns, quarter // 2))
    mine = mine.reshape(2 * n_z, own_columns, quarter // 2)
    block = lax.all_to_all(mine, ("xl", "z"), 0, 0, tiled=True)
    block = block.reshape(2 * n_z * own_columns, quarter // 2)
    block = jnp.broadcast_to(block, (n_y, *block.shape))
    weight = lax.all_to_all(block, "y", 0, 0, tiled=True)
    weight = weight.reshape(-1, quarter // 2)

    term = pl.pallas_call(
        weight_kernel,
        out_shape=jax.ShapeDtypeStruct((n_y, wide // n_y, columns), jnp.bfloat16),
        in_specs=[in_smem(), in_vmem(), in_vmem(), in_vmem()],
        out_specs=in_vmem(),
        compiler_params=PARAMS,
    )(place, inputs, received, scaled)
    both = jnp.concatenate([scaled, received[:, wide:]])
    term, weight, both = lax.optimization_barrier((term, weight, both))
    terms = lax.all_to_all(term, "y", 0, 0, tiled=True)
    from_core = lax.ppermute(both, "c", SWAP)
    from_far = lax.ppermute(both, "xh", SWAP)
    from_both = lax.ppermute(both, TP, [(i, i ^ 3) for i in range(n_tp)])
    ordered = pl.pallas_call(
        functools.partial(order_kernel, (n_z, n_y, own_columns)),
        out_shape=jax.ShapeDtypeStruct((2 * rows, n_tp * columns), jnp.bfloat16),
        in_specs=[in_smem(), in_vmem(), in_vmem(), in_vmem(), in_vmem()],
        out_specs=in_vmem(),
        compiler_params=PARAMS,
    )(place, both, from_core, from_far, from_both)
    kept, sent = pl.pallas_call(
        input_kernel,
        out_shape=[jax.ShapeDtypeStruct((rows, quarter // 2), jnp.bfloat16)] * 2,
        in_specs=[in_vmem(), in_vmem()],
        out_specs=[in_vmem(), in_vmem()],
        compiler_params=PARAMS,
    )(ordered, weight)
    terms, sent = lax.optimization_barrier((terms, sent))
    summed = jnp.sum(terms.astype(jnp.float32), axis=0)
    summed = summed.reshape(n_z, -1, columns)
    summed = lax.all_to_all(summed, "z", 0, 0, tiled=True)
    normalizer = 1.0 / math.sqrt(counts.shape[1] * lax.axis_size(FSDP))
    weight_grad = jnp.sum(summed, axis=0) * normalizer
    other = lax.ppermute(sent, "xl", SWAP)
    low = jnp.where(half == 0, kept, other)
    high = jnp.where(half == 0, other, kept)
    input_grad = jnp.concatenate([low, high], axis=1)
    return (input_grad, weight_grad)


def solution(mesh):
    split = Mesh(mesh.devices.reshape(16, 2, 8, 2, 2), (*FSDP, *TP))
    in_specs = (P(FSDP, None), P(FSDP, TP), P(TP, FSDP), P(FSDP, None), P(FSDP, None))
    out_specs = (P(FSDP, TP), P(FSDP, TP))
    return jax.shard_map(local, mesh=split, in_specs=in_specs, out_specs=out_specs, check_vma=False)
```

```python
import functools
import math

import jax
import jax.numpy as jnp
from jax import lax
from jax.experimental import pallas as pl
from jax.experimental.pallas import tpu as pltpu
from jax.sharding import Mesh
from jax.sharding import PartitionSpec as P

FSDP = ("zh", "zl", "xl", "y")
TP = ("xh", "c")
SWAP = [(0, 1), (1, 0)]
BOTH = [(i, i ^ 3) for i in range(4)]
MIB = 1024 * 1024


def prep_kernel(place_ref, counts_ref, offsets_ref, grad_ref, inputs_ref, *outs):
    q = place_ref[0]
    rows, columns = grad_ref.shape
    blocks = (outs[0].shape[1] - columns) // 128
    positions = lax.broadcasted_iota(jnp.int32, (rows, columns), 0)
    length = jnp.zeros((rows, columns), jnp.int32)
    for s in range(counts_ref.shape[1]):
        first = offsets_ref[0, s]
        count = counts_ref[0, s]
        length = jnp.where((positions >= first) & (positions < first + count), count, length)
    factor = jnp.where(length > 0, lax.rsqrt(jnp.maximum(length, 1).astype(jnp.float32)), 0.0)
    scaled = (grad_ref[...].astype(jnp.float32) * factor).astype(jnp.bfloat16)
    for m, out_ref in enumerate(outs):
        target = q ^ m
        for b in range(blocks):
            source = pl.ds(pl.multiple_of((4 * b + target) * 128, 128), 128)
            out_ref[:, b * 128 : (b + 1) * 128] = inputs_ref[:, source]
        out_ref[:, blocks * 128 :] = scaled


def weight_kernel(*refs):
    parts, out_ref = refs[:4], refs[4]
    peers, _, columns = out_ref.shape
    wide = parts[0].shape[1] - columns
    each = 128 // peers
    for b in range(wide // 128):
        term = None
        for part in parts:
            product = lax.dot_general(
                part[:, b * 128 : (b + 1) * 128],
                part[:, wide:],
                (((0,), (0,)), ((), ())),
                preferred_element_type=jnp.float32,
            )
            term = product if term is None else term + product
        out_ref[:, b * each : (b + 1) * each, :] = term.reshape(peers, each, -1).astype(jnp.bfloat16)


def order_kernel(sizes, place_ref, own_ref, core_ref, far_ref, both_ref, out_ref):
    tensor = place_ref[1]
    parts = [own_ref, core_ref, far_ref, both_ref]
    wide = own_ref.shape[1]
    n_z, n_y, n_j = sizes
    total = len(parts) * wide
    spot = lax.broadcasted_iota(jnp.int32, (1, total), 1)
    j = spot % n_j
    z = (spot // n_j) % n_z
    xl = (spot // (n_j * n_z)) % 2
    y = spot // (n_j * n_z * 2)
    source = ((z * 2 + xl) * n_y + y) * n_j + j
    for c in range(0, total, 256):
        moved = None
        for p, part in enumerate(parts):
            row = lax.broadcasted_iota(jnp.int32, (wide, 256), 0) + (tensor ^ p) * wide
            pick = (row == source[:, c : c + 256]).astype(jnp.float32).astype(jnp.bfloat16)
            term = jnp.dot(part[...], pick, preferred_element_type=jnp.float32)
            moved = term if moved is None else moved + term
        out_ref[:, c : c + 256] = moved.astype(jnp.bfloat16)


def input_kernel(scaled_ref, weight_ref, *outs):
    rows = outs[0].shape[0]
    for m, out_ref in enumerate(outs):
        out_ref[...] = jnp.dot(
            scaled_ref[m * rows : (m + 1) * rows, :],
            weight_ref[...],
            preferred_element_type=jnp.float32,
        ).astype(jnp.bfloat16)


def join_kernel(place_ref, *refs):
    parts, out_ref = refs[:4], refs[4]
    wide = parts[0].shape[1]
    for m, part in enumerate(parts):
        place = pl.multiple_of((place_ref[0] ^ m) * wide, 128)
        out_ref[:, pl.ds(place, wide)] = part[...]


def call(kernel, outs, n_smem, *args, vmem=24 * MIB):
    shapes = [jax.ShapeDtypeStruct(shape, jnp.bfloat16) for shape in outs]
    spaces = [pltpu.SMEM] * n_smem + [pltpu.VMEM] * (len(args) - n_smem)
    return pl.pallas_call(
        kernel,
        out_shape=shapes,
        in_specs=[pl.BlockSpec(memory_space=space) for space in spaces],
        out_specs=[pl.BlockSpec(memory_space=pltpu.VMEM)] * len(outs),
        compiler_params=pltpu.CompilerParams(vmem_limit_bytes=vmem),
    )(*args)


def from_group(blocks):
    return [
        blocks[0],
        lax.ppermute(blocks[1], "xl", SWAP),
        lax.ppermute(blocks[2], "zl", SWAP),
        lax.ppermute(blocks[3], ("zl", "xl"), BOTH),
    ]


def local(inputs, value_grad, value_weight, counts, offsets):
    rows, features = inputs.shape
    columns = value_grad.shape[1]
    quarter, own_columns = value_weight.shape
    n_tp, n_y, n_zh = (lax.axis_size(a) for a in (TP, "y", "zh"))
    wide = features // 4
    narrow = quarter // 4

    place = jnp.stack([lax.axis_index(("zl", "xl")), lax.axis_index(TP)]).astype(jnp.int32)
    args = (place, counts, offsets, value_grad, inputs)
    blocks = call(prep_kernel, [(rows, wide + columns)] * 4, 3, *args, vmem=60 * MIB)
    blocks, value_weight = lax.optimization_barrier((blocks, value_weight))
    received = from_group(blocks)

    mine = value_weight.T.reshape(own_columns, 2, 2, narrow).transpose(2, 1, 0, 3)
    mine = jnp.broadcast_to(mine[:, None], (2, n_zh, 2, own_columns, narrow))
    mine = mine.reshape(-1, own_columns, narrow)
    block = lax.all_to_all(mine, ("xl", "zh", "zl"), 0, 0, tiled=True)
    received, block = lax.optimization_barrier((received, block))
    block = block.reshape(-1, narrow)
    block = jnp.broadcast_to(block, (n_y, *block.shape))
    weight = lax.all_to_all(block, "y", 0, 0, tiled=True).reshape(-1, narrow)

    (term,) = call(weight_kernel, [(n_y, wide // n_y, columns)], 0, *received)
    own = jnp.concatenate([part[:, wide:] for part in received])
    gathered = [
        own,
        lax.ppermute(own, "c", SWAP),
        lax.ppermute(own, "xh", SWAP),
        lax.ppermute(own, TP, BOTH),
    ]
    term, weight, gathered = lax.optimization_barrier((term, weight, gathered))
    terms = lax.all_to_all(term, "y", 0, 0, tiled=True)

    sizes = (2 * n_zh, n_y, own_columns)
    kernel = functools.partial(order_kernel, sizes)
    (ordered,) = call(kernel, [(4 * rows, n_tp * columns)], 1, place, *gathered)
    outs = call(input_kernel, [(rows, narrow)] * 4, 0, ordered, weight)

    terms, outs = lax.optimization_barrier((terms, outs))
    summed = jnp.sum(terms.astype(jnp.float32), axis=0).reshape(n_zh, -1, columns)
    summed = lax.all_to_all(summed, "zh", 0, 0, tiled=True)
    normalizer = 1.0 / math.sqrt(counts.shape[1] * lax.axis_size(FSDP))
    weight_grad = jnp.sum(summed, axis=0) * normalizer

    (input_grad,) = call(join_kernel, [(rows, quarter)], 1, place, *from_group(outs))
    return (input_grad, weight_grad)


def solution(mesh):
    split = Mesh(mesh.devices.reshape(8, 2, 2, 8, 2, 2), (*FSDP, *TP))
    in_specs = (P(FSDP, None), P(FSDP, TP), P(TP, FSDP), P(FSDP, None), P(FSDP, None))
    out_specs = (P(FSDP, TP), P(FSDP, TP))
    return jax.shard_map(local, mesh=split, in_specs=in_specs, out_specs=out_specs, check_vma=False)
```

```python
import math

import jax
import jax.numpy as jnp
from jax import lax
from jax.experimental import pallas as pl
from jax.experimental.pallas import tpu as pltpu
from jax.sharding import Mesh
from jax.sharding import PartitionSpec as P

FSDP = ("zh", "zl", "xl", "y")
TP = ("xh", "c")
SWAP = [(0, 1), (1, 0)]
BOTH = [(i, i ^ 3) for i in range(4)]
MIB = 1024 * 1024


def prep_kernel(place_ref, counts_ref, offsets_ref, grad_ref, inputs_ref, *outs):
    q = place_ref[0]
    rows, columns = grad_ref.shape
    blocks = (outs[0].shape[1] - columns) // 128
    positions = lax.broadcasted_iota(jnp.int32, (rows, columns), 0)
    length = jnp.zeros((rows, columns), jnp.int32)
    for s in range(counts_ref.shape[1]):
        first = offsets_ref[0, s]
        count = counts_ref[0, s]
        length = jnp.where((positions >= first) & (positions < first + count), count, length)
    factor = jnp.where(length > 0, lax.rsqrt(jnp.maximum(length, 1).astype(jnp.float32)), 0.0)
    scaled = (grad_ref[...].astype(jnp.float32) * factor).astype(jnp.bfloat16)
    for m, out_ref in enumerate(outs):
        target = q ^ m
        for b in range(blocks):
            source = pl.ds(pl.multiple_of((4 * b + target) * 128, 128), 128)
            out_ref[:, b * 128 : (b + 1) * 128] = inputs_ref[:, source]
        out_ref[:, blocks * 128 :] = scaled


def weight_kernel(place_ref, *refs):
    parts, outs, terms = refs[:4], refs[4:-1], refs[-1]
    peers, _, columns = terms.shape
    wide = parts[0].shape[1] - columns
    each = 128 // peers
    for b in range(wide // 128):
        term = None
        for part in parts:
            product = lax.dot_general(
                part[:, b * 128 : (b + 1) * 128],
                part[:, wide:],
                (((0,), (0,)), ((), ())),
                preferred_element_type=jnp.float32,
            )
            term = product if term is None else term + product
        terms[:, b * each : (b + 1) * each, :] = term.reshape(peers, each, -1).astype(jnp.bfloat16)
    for m, out_ref in enumerate(outs):
        out_ref[...] = terms[(place_ref[2] + m) % peers]


def sum_kernel(*refs):
    parts, out_ref = refs[:-1], refs[-1]
    total = parts[0][...].astype(jnp.float32)
    for part in parts[1:]:
        total += part[...].astype(jnp.float32)
    out_ref[...] = total


def input_kernel(place_ref, *refs):
    parts, weight_ref, outs = refs[:4], refs[4], refs[5:]
    rows, wide = outs[0].shape[0], parts[0].shape[1]
    for m, out_ref in enumerate(outs):
        total = None
        for p, part in enumerate(parts):
            place = pl.multiple_of((place_ref[1] ^ p) * wide, wide)
            term = jnp.dot(
                part[m * rows : (m + 1) * rows, :],
                weight_ref[pl.ds(place, wide), :],
                preferred_element_type=jnp.float32,
            )
            total = term if total is None else total + term
        out_ref[...] = total.astype(jnp.bfloat16)


def join_kernel(place_ref, *refs):
    parts, out_ref = refs[:4], refs[4]
    wide = parts[0].shape[1]
    for m, part in enumerate(parts):
        place = pl.multiple_of((place_ref[0] ^ m) * wide, 128)
        out_ref[:, pl.ds(place, wide)] = part[...]


def call(kernel, outs, n_smem, *args, vmem=24 * MIB, dtype=jnp.bfloat16, scratch=()):
    shapes = [jax.ShapeDtypeStruct(shape, dtype) for shape in outs]
    spaces = [pltpu.SMEM] * n_smem + [pltpu.VMEM] * (len(args) - n_smem)
    return pl.pallas_call(
        kernel,
        out_shape=shapes,
        in_specs=[pl.BlockSpec(memory_space=space) for space in spaces],
        out_specs=[pl.BlockSpec(memory_space=pltpu.VMEM)] * len(outs),
        scratch_shapes=scratch,
        compiler_params=pltpu.CompilerParams(vmem_limit_bytes=vmem),
    )(*args)


def from_group(blocks):
    return [
        blocks[0],
        lax.ppermute(blocks[1], "xl", SWAP),
        lax.ppermute(blocks[2], "zl", SWAP),
        lax.ppermute(blocks[3], ("zl", "xl"), BOTH),
    ]


def local(inputs, value_grad, value_weight, counts, offsets):
    rows, features = inputs.shape
    columns = value_grad.shape[1]
    quarter, own_columns = value_weight.shape
    n_y, n_zh = (lax.axis_size(a) for a in ("y", "zh"))
    wide = features // 4
    narrow = quarter // 4

    place = [lax.axis_index(a) for a in (("zl", "xl"), TP, "y")]
    place = jnp.stack(place).astype(jnp.int32)
    args = (place, counts, offsets, value_grad, inputs)
    blocks = call(prep_kernel, [(rows, wide + columns)] * 4, 3, *args, vmem=60 * MIB)
    blocks, value_weight = lax.optimization_barrier((blocks, value_weight))
    received = from_group(blocks)

    mine = value_weight.T.reshape(own_columns, 2, 2, narrow).transpose(1, 2, 0, 3)
    mine = jnp.broadcast_to(mine[None, :, :, None], (n_zh, 2, 2, n_y, own_columns, narrow))
    mine = mine.reshape(-1, own_columns, narrow)
    weight = lax.all_to_all(mine, FSDP, 0, 0, tiled=True).reshape(-1, narrow)

    chunk = (wide // n_y, columns)
    scratch = [pltpu.VMEM((n_y, *chunk), jnp.bfloat16)]
    terms = list(call(weight_kernel, [chunk] * n_y, 1, place, *received, scratch=scratch))
    for m in range(1, n_y):
        terms[m] = lax.ppermute(terms[m], "y", [(i, (i + m) % n_y) for i in range(n_y)])

    own = jnp.concatenate([part[:, wide:] for part in received])
    own, terms[1] = lax.optimization_barrier((own, terms[1]))
    gathered = [
        own,
        lax.ppermute(own, "c", SWAP),
        lax.ppermute(own, "xh", SWAP),
        lax.ppermute(own, TP, BOTH),
    ]

    (summed,) = call(sum_kernel, [chunk], 0, *terms, dtype=jnp.float32)
    summed, weight = lax.optimization_barrier((summed, weight))
    summed = lax.all_to_all(summed.reshape(n_zh, -1, columns), "zh", 0, 0, tiled=True)
    normalizer = 1.0 / math.sqrt(counts.shape[1] * lax.axis_size(FSDP))
    weight_grad = jnp.sum(summed, axis=0) * normalizer

    outs = call(input_kernel, [(rows, narrow)] * 4, 1, place, *gathered, weight)
    (input_grad,) = call(join_kernel, [(rows, quarter)], 1, place, *from_group(outs))
    return (input_grad, weight_grad)


def solution(mesh):
    split = Mesh(mesh.devices.reshape(8, 2, 2, 8, 2, 2), (*FSDP, *TP))
    in_specs = (P(FSDP, None), P(FSDP, TP), P(TP, FSDP), P(FSDP, None), P(FSDP, None))
    out_specs = (P(FSDP, TP), P(FSDP, TP))
    return jax.shard_map(local, mesh=split, in_specs=in_specs, out_specs=out_specs, check_vma=False)
```

```python
import functools
import math

import jax
import jax.numpy as jnp
from jax import lax
from jax.experimental import pallas as pl
from jax.experimental.pallas import tpu as pltpu
from jax.sharding import Mesh
from jax.sharding import PartitionSpec as P

FSDP = ("zh", "zl", "xl", "y")
TP = ("xh", "c")
SWAP = [(0, 1), (1, 0)]
BOTH = [(i, i ^ 3) for i in range(4)]
MIB = 1024 * 1024


def prep_kernel(place_ref, counts_ref, offsets_ref, grad_ref, inputs_ref, *outs):
    q = place_ref[0]
    rows, columns = grad_ref.shape
    blocks = (outs[0].shape[1] - columns) // 128
    positions = lax.broadcasted_iota(jnp.int32, (rows, columns), 0)
    length = jnp.zeros((rows, columns), jnp.int32)
    for s in range(counts_ref.shape[1]):
        first = offsets_ref[0, s]
        count = counts_ref[0, s]
        length = jnp.where((positions >= first) & (positions < first + count), count, length)
    factor = jnp.where(length > 0, lax.rsqrt(jnp.maximum(length, 1).astype(jnp.float32)), 0.0)
    scaled = (grad_ref[...].astype(jnp.float32) * factor).astype(jnp.bfloat16)
    for m, out_ref in enumerate(outs):
        target = q ^ m
        for b in range(blocks):
            source = pl.ds(pl.multiple_of((4 * b + target) * 128, 128), 128)
            out_ref[:, b * 128 : (b + 1) * 128] = inputs_ref[:, source]
        out_ref[:, blocks * 128 :] = scaled


def weight_kernel(*refs):
    parts, out_ref = refs[:4], refs[4]
    peers, _, columns = out_ref.shape
    wide = parts[0].shape[1] - columns
    each = 128 // peers
    for b in range(wide // 128):
        term = None
        for part in parts:
            product = lax.dot_general(
                part[:, b * 128 : (b + 1) * 128],
                part[:, wide:],
                (((0,), (0,)), ((), ())),
                preferred_element_type=jnp.float32,
            )
            term = product if term is None else term + product
        out_ref[:, b * each : (b + 1) * each, :] = term.reshape(peers, each, -1).astype(jnp.bfloat16)


def order_kernel(sizes, place_ref, own_ref, core_ref, far_ref, both_ref, out_ref):
    tensor = place_ref[1]
    parts = [own_ref, core_ref, far_ref, both_ref]
    wide = own_ref.shape[1]
    n_z, n_y, n_j = sizes
    total = len(parts) * wide
    spot = lax.broadcasted_iota(jnp.int32, (1, total), 1)
    j = spot % n_j
    z = (spot // n_j) % n_z
    xl = (spot // (n_j * n_z)) % 2
    y = spot // (n_j * n_z * 2)
    source = ((z * 2 + xl) * n_y + y) * n_j + j
    for c in range(0, total, 256):
        moved = None
        for p, part in enumerate(parts):
            row = lax.broadcasted_iota(jnp.int32, (wide, 256), 0) + (tensor ^ p) * wide
            pick = (row == source[:, c : c + 256]).astype(jnp.float32).astype(jnp.bfloat16)
            term = jnp.dot(part[...], pick, preferred_element_type=jnp.float32)
            moved = term if moved is None else moved + term
        out_ref[:, c : c + 256] = moved.astype(jnp.bfloat16)


def input_kernel(scaled_ref, weight_ref, *outs):
    rows = outs[0].shape[0]
    for m, out_ref in enumerate(outs):
        out_ref[...] = jnp.dot(
            scaled_ref[m * rows : (m + 1) * rows, :],
            weight_ref[...],
            preferred_element_type=jnp.float32,
        ).astype(jnp.bfloat16)


def join_kernel(place_ref, *refs):
    parts, out_ref = refs[:4], refs[4]
    wide = parts[0].shape[1]
    for m, part in enumerate(parts):
        place = pl.multiple_of((place_ref[0] ^ m) * wide, 128)
        out_ref[:, pl.ds(place, wide)] = part[...]


def call(kernel, outs, n_smem, *args, vmem=24 * MIB):
    shapes = [jax.ShapeDtypeStruct(shape, jnp.bfloat16) for shape in outs]
    spaces = [pltpu.SMEM] * n_smem + [pltpu.VMEM] * (len(args) - n_smem)
    return pl.pallas_call(
        kernel,
        out_shape=shapes,
        in_specs=[pl.BlockSpec(memory_space=space) for space in spaces],
        out_specs=[pl.BlockSpec(memory_space=pltpu.VMEM)] * len(outs),
        compiler_params=pltpu.CompilerParams(vmem_limit_bytes=vmem),
    )(*args)


def from_group(blocks):
    return [
        blocks[0],
        lax.ppermute(blocks[1], "xl", SWAP),
        lax.ppermute(blocks[2], "zl", SWAP),
        lax.ppermute(blocks[3], ("zl", "xl"), BOTH),
    ]


def local(inputs, value_grad, value_weight, counts, offsets):
    rows, features = inputs.shape
    columns = value_grad.shape[1]
    quarter, own_columns = value_weight.shape
    n_tp, n_y, n_zh = (lax.axis_size(a) for a in (TP, "y", "zh"))
    wide = features // 4
    narrow = quarter // 4

    place = jnp.stack([lax.axis_index(("zl", "xl")), lax.axis_index(TP)]).astype(jnp.int32)
    args = (place, counts, offsets, value_grad, inputs)
    blocks = call(prep_kernel, [(rows, wide + columns)] * 4, 3, *args, vmem=60 * MIB)
    blocks, value_weight = lax.optimization_barrier((blocks, value_weight))
    received = from_group(blocks)

    mine = value_weight.T.reshape(own_columns, 2, 2, narrow).transpose(2, 1, 0, 3)
    mine = jnp.broadcast_to(mine[:, None], (2, n_zh, 2, own_columns, narrow))
    mine = mine.reshape(-1, own_columns, narrow)
    block = lax.all_to_all(mine, ("xl", "zh", "zl"), 0, 0, tiled=True)
    received, block = lax.optimization_barrier((received, block))
    block = block.reshape(-1, narrow)
    block = jnp.broadcast_to(block, (n_y, *block.shape))
    weight = lax.all_to_all(block, "y", 0, 0, tiled=True).reshape(-1, narrow)

    (term,) = call(weight_kernel, [(n_y, wide // n_y, columns)], 0, *received)
    own = jnp.concatenate([part[:, wide:] for part in received])
    gathered = [
        own,
        lax.ppermute(own, "c", SWAP),
        lax.ppermute(own, "xh", SWAP),
        lax.ppermute(own, TP, BOTH),
    ]
    term, weight, gathered[1] = lax.optimization_barrier((term, weight, gathered[1]))
    terms = lax.all_to_all(term, "y", 0, 0, tiled=True)

    sizes = (2 * n_zh, n_y, own_columns)
    kernel = functools.partial(order_kernel, sizes)
    (ordered,) = call(kernel, [(4 * rows, n_tp * columns)], 1, place, *gathered)
    outs = call(input_kernel, [(rows, narrow)] * 4, 0, ordered, weight)

    summed = jnp.sum(terms.astype(jnp.float32), axis=0).reshape(n_zh, -1, columns)
    summed = lax.all_to_all(summed, "zh", 0, 0, tiled=True)
    normalizer = 1.0 / math.sqrt(counts.shape[1] * lax.axis_size(FSDP))
    weight_grad = jnp.sum(summed, axis=0) * normalizer

    (input_grad,) = call(join_kernel, [(rows, quarter)], 1, place, *from_group(outs))
    return (input_grad, weight_grad)


def solution(mesh):
    split = Mesh(mesh.devices.reshape(8, 2, 2, 8, 2, 2), (*FSDP, *TP))
    in_specs = (P(FSDP, None), P(FSDP, TP), P(TP, FSDP), P(FSDP, None), P(FSDP, None))
    out_specs = (P(FSDP, TP), P(FSDP, TP))
    return jax.shard_map(local, mesh=split, in_specs=in_specs, out_specs=out_specs, check_vma=False)
```

```python
import functools
import math

import jax
import jax.numpy as jnp
from jax import lax
from jax.experimental import pallas as pl
from jax.experimental.pallas import tpu as pltpu
from jax.sharding import Mesh
from jax.sharding import PartitionSpec as P

FSDP = ("zh", "zl", "xl", "y")
TP = ("xh", "c")
SWAP = [(0, 1), (1, 0)]
BOTH = [(i, i ^ 3) for i in range(4)]
MIB = 1024 * 1024


def prep_kernel(place_ref, counts_ref, offsets_ref, grad_ref, inputs_ref, own_ref, *outs):
    q, core = place_ref[0], place_ref[2]
    rows, columns = grad_ref.shape
    wide = own_ref.shape[1] - columns
    short = rows // 2
    positions = lax.broadcasted_iota(jnp.int32, (rows, columns), 0)
    length = jnp.zeros((rows, columns), jnp.int32)
    for s in range(counts_ref.shape[1]):
        first = offsets_ref[0, s]
        count = counts_ref[0, s]
        length = jnp.where((positions >= first) & (positions < first + count), count, length)
    factor = jnp.where(length > 0, lax.rsqrt(jnp.maximum(length, 1).astype(jnp.float32)), 0.0)
    scaled = (grad_ref[...].astype(jnp.float32) * factor).astype(jnp.bfloat16)
    own_ref[:, wide:] = scaled
    mine = pl.ds(pl.multiple_of(core * short, short), short)
    other = pl.ds(pl.multiple_of((1 - core) * short, short), short)
    for b in range(wide // 128):
        source = pl.ds(pl.multiple_of((4 * b + q) * 128, 128), 128)
        own_ref[:, b * 128 : (b + 1) * 128] = inputs_ref[:, source]
    for m, out_ref in enumerate(outs, 1):
        for b in range(wide // 128):
            source = pl.ds(pl.multiple_of((4 * b + (q ^ m)) * 128, 128), 128)
            out_ref[:, b * 128 : (b + 1) * 128] = inputs_ref[mine, source]
        out_ref[:, wide : wide + columns] = own_ref[mine, wide:]
        out_ref[:, wide + columns :] = own_ref[other, wide:]


def split_kernel(place_ref, own_ref, *refs):
    parts, half_ref, scaled_ref = refs[:3], refs[3], refs[4]
    core = place_ref[2]
    short, wide = parts[0].shape[0], half_ref.shape[1]
    columns = scaled_ref.shape[1]
    scaled_ref[: 2 * short, :] = own_ref[:, wide:]
    for m, part in enumerate(parts, 1):
        half_ref[(m - 1) * short : m * short, :] = part[:, :wide]
        mine = pl.ds(pl.multiple_of((2 * m + core) * short, short), short)
        other = pl.ds(pl.multiple_of((2 * m + 1 - core) * short, short), short)
        scaled_ref[mine, :] = part[:, wide : wide + columns]
        scaled_ref[other, :] = part[:, wide + columns :]


def weight_kernel(own_ref, *refs):
    parts, half_ref, out_ref = refs[:3], refs[3], refs[4]
    peers, _, columns = out_ref.shape
    wide = half_ref.shape[1]
    short = parts[0].shape[0]
    each = 128 // peers

    def product(left, right):
        dims = (((0,), (0,)), ((), ()))
        return lax.dot_general(left, right, dims, preferred_element_type=jnp.float32)

    for b in range(wide // 128):
        block = slice(b * 128, (b + 1) * 128)
        term = product(own_ref[:, block], own_ref[:, wide:])
        for m, part in enumerate(parts):
            term += product(part[:, block], part[:, wide : wide + columns])
            term += product(half_ref[m * short : (m + 1) * short, block], part[:, wide + columns :])
        out_ref[:, b * each : (b + 1) * each, :] = term.reshape(peers, each, -1).astype(jnp.bfloat16)


def order_kernel(sizes, place_ref, own_ref, core_ref, far_ref, both_ref, out_ref):
    tensor = place_ref[1]
    parts = [own_ref, core_ref, far_ref, both_ref]
    wide = own_ref.shape[1]
    n_z, n_y, n_j = sizes
    total = len(parts) * wide
    spot = lax.broadcasted_iota(jnp.int32, (1, total), 1)
    j = spot % n_j
    z = (spot // n_j) % n_z
    xl = (spot // (n_j * n_z)) % 2
    y = spot // (n_j * n_z * 2)
    source = ((z * 2 + xl) * n_y + y) * n_j + j
    for c in range(0, total, 256):
        moved = None
        for p, part in enumerate(parts):
            row = lax.broadcasted_iota(jnp.int32, (wide, 256), 0) + (tensor ^ p) * wide
            pick = (row == source[:, c : c + 256]).astype(jnp.float32).astype(jnp.bfloat16)
            term = jnp.dot(part[...], pick, preferred_element_type=jnp.float32)
            moved = term if moved is None else moved + term
        out_ref[:, c : c + 256] = moved.astype(jnp.bfloat16)


def input_kernel(scaled_ref, weight_ref, *outs):
    rows = outs[0].shape[0]
    for m, out_ref in enumerate(outs):
        out_ref[...] = jnp.dot(
            scaled_ref[m * rows : (m + 1) * rows, :],
            weight_ref[...],
            preferred_element_type=jnp.float32,
        ).astype(jnp.bfloat16)


def join_kernel(place_ref, *refs):
    parts, out_ref = refs[:4], refs[4]
    wide = parts[0].shape[1]
    for m, part in enumerate(parts):
        place = pl.multiple_of((place_ref[0] ^ m) * wide, 128)
        out_ref[:, pl.ds(place, wide)] = part[...]


def call(kernel, outs, n_smem, *args, vmem=24 * MIB):
    shapes = [jax.ShapeDtypeStruct(shape, jnp.bfloat16) for shape in outs]
    spaces = [pltpu.SMEM] * n_smem + [pltpu.VMEM] * (len(args) - n_smem)
    return pl.pallas_call(
        kernel,
        out_shape=shapes,
        in_specs=[pl.BlockSpec(memory_space=space) for space in spaces],
        out_specs=[pl.BlockSpec(memory_space=pltpu.VMEM)] * len(outs),
        compiler_params=pltpu.CompilerParams(vmem_limit_bytes=vmem),
    )(*args)


def from_group(blocks):
    return [
        blocks[0],
        lax.ppermute(blocks[1], "xl", SWAP),
        lax.ppermute(blocks[2], "zl", SWAP),
        lax.ppermute(blocks[3], ("zl", "xl"), BOTH),
    ]


def local(inputs, value_grad, value_weight, counts, offsets):
    rows, features = inputs.shape
    columns = value_grad.shape[1]
    quarter, own_columns = value_weight.shape
    n_tp, n_y, n_zh = (lax.axis_size(a) for a in (TP, "y", "zh"))
    wide = features // 4
    narrow = quarter // 4

    place = jnp.stack([lax.axis_index(a) for a in (("zl", "xl"), TP, "c")]).astype(jnp.int32)
    args = (place, counts, offsets, value_grad, inputs)
    sizes = [(rows, wide + columns)] + [(rows // 2, wide + 2 * columns)] * 3
    blocks = call(prep_kernel, sizes, 3, *args, vmem=60 * MIB)
    blocks, value_weight = lax.optimization_barrier((blocks, value_weight))
    received = from_group(blocks)

    mine = value_weight.T.reshape(own_columns, 2, 2, narrow).transpose(2, 1, 0, 3)
    mine = jnp.broadcast_to(mine[:, None], (2, n_zh, 2, own_columns, narrow))
    mine = mine.reshape(-1, own_columns, narrow)
    block = lax.all_to_all(mine, ("xl", "zh", "zl"), 0, 0, tiled=True)
    received, block = lax.optimization_barrier((received, block))
    block = block.reshape(-1, narrow)
    block = jnp.broadcast_to(block, (n_y, *block.shape))
    weight = lax.all_to_all(block, "y", 0, 0, tiled=True).reshape(-1, narrow)

    sizes = [(3 * rows // 2, wide), (4 * rows, columns)]
    half, own = call(split_kernel, sizes, 1, place, *received)
    half = lax.ppermute(half, "c", SWAP)
    from_far = lax.ppermute(own, "xh", SWAP)
    from_core = lax.ppermute(own, "c", SWAP)
    (term,) = call(weight_kernel, [(n_y, wide // n_y, columns)], 0, *received, half)
    early = (term, weight, from_far, from_core)
    term, weight, from_far, from_core = lax.optimization_barrier(early)
    terms = lax.all_to_all(term, "y", 0, 0, tiled=True)
    gathered = [own, from_core, from_far, lax.ppermute(from_far, "c", SWAP)]

    sizes = (2 * n_zh, n_y, own_columns)
    kernel = functools.partial(order_kernel, sizes)
    (ordered,) = call(kernel, [(4 * rows, n_tp * columns)], 1, place, *gathered)
    outs = call(input_kernel, [(rows, narrow)] * 4, 0, ordered, weight)

    terms, outs = lax.optimization_barrier((terms, outs))
    summed = jnp.sum(terms.astype(jnp.float32), axis=0).reshape(n_zh, -1, columns)
    summed = lax.all_to_all(summed, "zh", 0, 0, tiled=True)
    normalizer = 1.0 / math.sqrt(counts.shape[1] * lax.axis_size(FSDP))
    weight_grad = jnp.sum(summed, axis=0) * normalizer

    (input_grad,) = call(join_kernel, [(rows, quarter)], 1, place, *from_group(outs))
    return (input_grad, weight_grad)


def solution(mesh):
    split = Mesh(mesh.devices.reshape(8, 2, 2, 8, 2, 2), (*FSDP, *TP))
    in_specs = (P(FSDP, None), P(FSDP, TP), P(TP, FSDP), P(FSDP, None), P(FSDP, None))
    out_specs = (P(FSDP, TP), P(FSDP, TP))
    return jax.shard_map(local, mesh=split, in_specs=in_specs, out_specs=out_specs, check_vma=False)
```

```python
import functools
import math

import jax
import jax.numpy as jnp
from jax import lax
from jax.experimental import pallas as pl
from jax.experimental.pallas import tpu as pltpu
from jax.sharding import Mesh
from jax.sharding import PartitionSpec as P

FSDP = ("zh", "zl", "xl", "y")
TP = ("xh", "c")
SWAP = [(0, 1), (1, 0)]
BOTH = [(i, i ^ 3) for i in range(4)]
MIB = 1024 * 1024


def prep_kernel(place_ref, counts_ref, offsets_ref, grad_ref, inputs_ref, own_ref, *outs):
    q, core = place_ref[0], place_ref[2]
    rows, columns = grad_ref.shape
    wide = own_ref.shape[1] - columns
    short = rows // 2
    positions = lax.broadcasted_iota(jnp.int32, (rows, columns), 0)
    length = jnp.zeros((rows, columns), jnp.int32)
    for s in range(counts_ref.shape[1]):
        first = offsets_ref[0, s]
        count = counts_ref[0, s]
        length = jnp.where((positions >= first) & (positions < first + count), count, length)
    factor = jnp.where(length > 0, lax.rsqrt(jnp.maximum(length, 1).astype(jnp.float32)), 0.0)
    scaled = (grad_ref[...].astype(jnp.float32) * factor).astype(jnp.bfloat16)
    own_ref[:, wide:] = scaled
    mine = pl.ds(pl.multiple_of(core * short, short), short)
    other = pl.ds(pl.multiple_of((1 - core) * short, short), short)
    for b in range(wide // 128):
        source = pl.ds(pl.multiple_of((4 * b + q) * 128, 128), 128)
        own_ref[:, b * 128 : (b + 1) * 128] = inputs_ref[:, source]
    for m, out_ref in enumerate(outs, 1):
        for b in range(wide // 128):
            source = pl.ds(pl.multiple_of((4 * b + (q ^ m)) * 128, 128), 128)
            out_ref[:, b * 128 : (b + 1) * 128] = inputs_ref[mine, source]
        out_ref[:, wide : wide + columns] = own_ref[mine, wide:]
        out_ref[:, wide + columns :] = own_ref[other, wide:]


def split_kernel(place_ref, own_ref, *refs):
    parts, half_ref, scaled_ref = refs[:3], refs[3], refs[4]
    core = place_ref[2]
    short, wide = parts[0].shape[0], half_ref.shape[1]
    columns = scaled_ref.shape[1]
    scaled_ref[: 2 * short, :] = own_ref[:, wide:]
    for m, part in enumerate(parts, 1):
        half_ref[(m - 1) * short : m * short, :] = part[:, :wide]
        mine = pl.ds(pl.multiple_of((2 * m + core) * short, short), short)
        other = pl.ds(pl.multiple_of((2 * m + 1 - core) * short, short), short)
        scaled_ref[mine, :] = part[:, wide : wide + columns]
        scaled_ref[other, :] = part[:, wide + columns :]


def weight_kernel(own_ref, *refs):
    parts, half_ref, out_ref = refs[:3], refs[3], refs[4]
    peers, _, columns = out_ref.shape
    wide = half_ref.shape[1]
    short = parts[0].shape[0]
    each = 128 // peers

    def product(left, right):
        dims = (((0,), (0,)), ((), ()))
        return lax.dot_general(left, right, dims, preferred_element_type=jnp.float32)

    for b in range(wide // 128):
        block = slice(b * 128, (b + 1) * 128)
        term = product(own_ref[:, block], own_ref[:, wide:])
        for m, part in enumerate(parts):
            term += product(part[:, block], part[:, wide : wide + columns])
            term += product(half_ref[m * short : (m + 1) * short, block], part[:, wide + columns :])
        out_ref[:, b * each : (b + 1) * each, :] = term.reshape(peers, each, -1).astype(jnp.bfloat16)


def order_kernel(sizes, place_ref, own_ref, core_ref, far_ref, both_ref, out_ref):
    tensor = place_ref[1]
    parts = [own_ref, core_ref, far_ref, both_ref]
    wide = own_ref.shape[1]
    n_z, n_y, n_j = sizes
    total = len(parts) * wide
    spot = lax.broadcasted_iota(jnp.int32, (1, total), 1)
    j = spot % n_j
    z = (spot // n_j) % n_z
    xl = (spot // (n_j * n_z)) % 2
    y = spot // (n_j * n_z * 2)
    source = ((z * 2 + xl) * n_y + y) * n_j + j
    for c in range(0, total, 256):
        moved = None
        for p, part in enumerate(parts):
            row = lax.broadcasted_iota(jnp.int32, (wide, 256), 0) + (tensor ^ p) * wide
            pick = (row == source[:, c : c + 256]).astype(jnp.float32).astype(jnp.bfloat16)
            term = jnp.dot(part[...], pick, preferred_element_type=jnp.float32)
            moved = term if moved is None else moved + term
        out_ref[:, c : c + 256] = moved.astype(jnp.bfloat16)


def input_kernel(scaled_ref, weight_ref, *outs):
    rows = outs[0].shape[0]
    for m, out_ref in enumerate(outs):
        out_ref[...] = jnp.dot(
            scaled_ref[m * rows : (m + 1) * rows, :],
            weight_ref[...],
            preferred_element_type=jnp.float32,
        ).astype(jnp.bfloat16)


def join_kernel(place_ref, *refs):
    parts, out_ref = refs[:4], refs[4]
    wide = parts[0].shape[1]
    for m, part in enumerate(parts):
        place = pl.multiple_of((place_ref[0] ^ m) * wide, 128)
        out_ref[:, pl.ds(place, wide)] = part[...]


def call(kernel, outs, n_smem, *args, vmem=24 * MIB):
    shapes = [jax.ShapeDtypeStruct(shape, jnp.bfloat16) for shape in outs]
    spaces = [pltpu.SMEM] * n_smem + [pltpu.VMEM] * (len(args) - n_smem)
    return pl.pallas_call(
        kernel,
        out_shape=shapes,
        in_specs=[pl.BlockSpec(memory_space=space) for space in spaces],
        out_specs=[pl.BlockSpec(memory_space=pltpu.VMEM)] * len(outs),
        compiler_params=pltpu.CompilerParams(vmem_limit_bytes=vmem),
    )(*args)


def from_group(blocks):
    return [
        blocks[0],
        lax.ppermute(blocks[1], "xl", SWAP),
        lax.ppermute(blocks[2], "zl", SWAP),
        lax.ppermute(blocks[3], ("zl", "xl"), BOTH),
    ]


def local(inputs, value_grad, value_weight, counts, offsets):
    rows, features = inputs.shape
    columns = value_grad.shape[1]
    quarter, own_columns = value_weight.shape
    n_tp, n_y, n_zh = (lax.axis_size(a) for a in (TP, "y", "zh"))
    wide = features // 4
    narrow = quarter // 4

    place = jnp.stack([lax.axis_index(a) for a in (("zl", "xl"), TP, "c")]).astype(jnp.int32)
    args = (place, counts, offsets, value_grad, inputs)
    sizes = [(rows, wide + columns)] + [(rows // 2, wide + 2 * columns)] * 3
    blocks = call(prep_kernel, sizes, 3, *args, vmem=60 * MIB)
    blocks, value_weight = lax.optimization_barrier((blocks, value_weight))
    received = from_group(blocks)

    mine = value_weight.T.reshape(own_columns, 2, 2, narrow).transpose(2, 1, 0, 3)
    mine = jnp.broadcast_to(mine[:, None], (2, n_zh, 2, own_columns, narrow))
    mine = mine.reshape(-1, own_columns, narrow)
    block = lax.all_to_all(mine, ("xl", "zh", "zl"), 0, 0, tiled=True)
    received, block = lax.optimization_barrier((received, block))
    block = block.reshape(-1, narrow)
    block = jnp.broadcast_to(block, (n_y, *block.shape))
    weight = lax.all_to_all(block, "y", 0, 0, tiled=True).reshape(-1, narrow)

    sizes = [(3 * rows // 2, wide), (4 * rows, columns)]
    half, own = call(split_kernel, sizes, 1, place, *received)
    from_far = lax.ppermute(own, "xh", SWAP)
    half = lax.ppermute(half, "c", SWAP)
    half, from_far = lax.optimization_barrier((half, from_far))
    from_core = lax.ppermute(own, "c", SWAP)
    (term,) = call(weight_kernel, [(n_y, wide // n_y, columns)], 0, *received, half)
    term, weight = lax.optimization_barrier((term, weight))
    terms = lax.all_to_all(term, "y", 0, 0, tiled=True)
    gathered = [own, from_core, from_far, lax.ppermute(from_far, "c", SWAP)]

    sizes = (2 * n_zh, n_y, own_columns)
    kernel = functools.partial(order_kernel, sizes)
    (ordered,) = call(kernel, [(4 * rows, n_tp * columns)], 1, place, *gathered)
    outs = call(input_kernel, [(rows, narrow)] * 4, 0, ordered, weight)

    outs = from_group(outs)
    terms, outs[1], outs[2] = lax.optimization_barrier((terms, outs[1], outs[2]))
    summed = jnp.sum(terms.astype(jnp.float32), axis=0).reshape(n_zh, -1, columns)
    summed = lax.all_to_all(summed, "zh", 0, 0, tiled=True)
    normalizer = 1.0 / math.sqrt(counts.shape[1] * lax.axis_size(FSDP))
    weight_grad = jnp.sum(summed, axis=0) * normalizer

    (input_grad,) = call(join_kernel, [(rows, quarter)], 1, place, *outs)
    return (input_grad, weight_grad)


def solution(mesh):
    split = Mesh(mesh.devices.reshape(8, 2, 2, 8, 2, 2), (*FSDP, *TP))
    in_specs = (P(FSDP, None), P(FSDP, TP), P(TP, FSDP), P(FSDP, None), P(FSDP, None))
    out_specs = (P(FSDP, TP), P(FSDP, TP))
    return jax.shard_map(local, mesh=split, in_specs=in_specs, out_specs=out_specs, check_vma=False)
```

```python
import functools
import math

import jax
import jax.numpy as jnp
from jax import lax
from jax.experimental import pallas as pl
from jax.experimental.pallas import tpu as pltpu
from jax.sharding import Mesh
from jax.sharding import PartitionSpec as P

FSDP = ("zh", "zl", "xl", "y")
TP = ("xh", "c")
SWAP = [(0, 1), (1, 0)]
BOTH = [(i, i ^ 3) for i in range(4)]
MIB = 1024 * 1024


def prep_kernel(place_ref, counts_ref, offsets_ref, grad_ref, inputs_ref, own_ref, *outs):
    q, core = place_ref[0], place_ref[2]
    rows, columns = grad_ref.shape
    wide = own_ref.shape[1] - columns
    short = rows // 2
    positions = lax.broadcasted_iota(jnp.int32, (rows, columns), 0)
    length = jnp.zeros((rows, columns), jnp.int32)
    for s in range(counts_ref.shape[1]):
        first = offsets_ref[0, s]
        count = counts_ref[0, s]
        length = jnp.where((positions >= first) & (positions < first + count), count, length)
    factor = jnp.where(length > 0, lax.rsqrt(jnp.maximum(length, 1).astype(jnp.float32)), 0.0)
    scaled = (grad_ref[...].astype(jnp.float32) * factor).astype(jnp.bfloat16)
    own_ref[:, wide:] = scaled
    mine = pl.ds(pl.multiple_of(core * short, short), short)
    other = pl.ds(pl.multiple_of((1 - core) * short, short), short)
    for b in range(wide // 128):
        source = pl.ds(pl.multiple_of((4 * b + q) * 128, 128), 128)
        own_ref[:, b * 128 : (b + 1) * 128] = inputs_ref[:, source]
    for m, out_ref in enumerate(outs, 1):
        for b in range(wide // 128):
            source = pl.ds(pl.multiple_of((4 * b + (q ^ m)) * 128, 128), 128)
            out_ref[:, b * 128 : (b + 1) * 128] = inputs_ref[mine, source]
        out_ref[:, wide : wide + columns] = own_ref[mine, wide:]
        out_ref[:, wide + columns :] = own_ref[other, wide:]


def split_kernel(place_ref, own_ref, *refs):
    parts, half_ref, scaled_ref = refs[:3], refs[3], refs[4]
    core = place_ref[2]
    short, wide = parts[0].shape[0], half_ref.shape[1]
    columns = scaled_ref.shape[1]
    scaled_ref[: 2 * short, :] = own_ref[:, wide:]
    for m, part in enumerate(parts, 1):
        half_ref[(m - 1) * short : m * short, :] = part[:, :wide]
        mine = pl.ds(pl.multiple_of((2 * m + core) * short, short), short)
        other = pl.ds(pl.multiple_of((2 * m + 1 - core) * short, short), short)
        scaled_ref[mine, :] = part[:, wide : wide + columns]
        scaled_ref[other, :] = part[:, wide + columns :]


def weight_kernel(own_ref, *refs):
    parts, half_ref, out_ref = refs[:3], refs[3], refs[4]
    peers, _, columns = out_ref.shape
    wide = half_ref.shape[1]
    short = parts[0].shape[0]
    each = 128 // peers

    def product(left, right):
        dims = (((0,), (0,)), ((), ()))
        return lax.dot_general(left, right, dims, preferred_element_type=jnp.float32)

    for b in range(wide // 128):
        block = slice(b * 128, (b + 1) * 128)
        term = product(own_ref[:, block], own_ref[:, wide:])
        for m, part in enumerate(parts):
            term += product(part[:, block], part[:, wide : wide + columns])
            term += product(half_ref[m * short : (m + 1) * short, block], part[:, wide + columns :])
        out_ref[:, b * each : (b + 1) * each, :] = term.reshape(peers, each, -1).astype(jnp.bfloat16)


def order_kernel(sizes, place_ref, own_ref, core_ref, far_ref, both_ref, out_ref):
    tensor = place_ref[1]
    parts = [own_ref, core_ref, far_ref, both_ref]
    wide = own_ref.shape[1]
    n_z, n_y, n_j = sizes
    total = len(parts) * wide
    spot = lax.broadcasted_iota(jnp.int32, (1, total), 1)
    j = spot % n_j
    z = (spot // n_j) % n_z
    xl = (spot // (n_j * n_z)) % 2
    flip = spot // (n_j * n_z * 2)
    y = place_ref[3] ^ ((flip % 2) * 4 + (flip // 2 % 2) * 2 + flip // 4)
    source = ((z * 2 + xl) * n_y + y) * n_j + j
    for c in range(0, total, 256):
        moved = None
        for p, part in enumerate(parts):
            row = lax.broadcasted_iota(jnp.int32, (wide, 256), 0) + (tensor ^ p) * wide
            pick = (row == source[:, c : c + 256]).astype(jnp.float32).astype(jnp.bfloat16)
            term = jnp.dot(part[...], pick, preferred_element_type=jnp.float32)
            moved = term if moved is None else moved + term
        out_ref[:, c : c + 256] = moved.astype(jnp.bfloat16)


def input_kernel(scaled_ref, near_ref, next_ref, *outs):
    rows, deep = outs[0].shape[0], near_ref.shape[0]
    for m, out_ref in enumerate(outs):
        block = slice(m * rows, (m + 1) * rows)
        total = jnp.dot(
            scaled_ref[block, :deep], near_ref[...], preferred_element_type=jnp.float32
        )
        total += jnp.dot(
            scaled_ref[block, deep:], next_ref[...], preferred_element_type=jnp.float32
        )
        out_ref[...] = total.astype(jnp.bfloat16)


def join_kernel(place_ref, *refs):
    parts, out_ref = refs[:4], refs[4]
    wide = parts[0].shape[1]
    for m, part in enumerate(parts):
        place = pl.multiple_of((place_ref[0] ^ m) * wide, 128)
        out_ref[:, pl.ds(place, wide)] = part[...]


def call(kernel, outs, n_smem, *args, vmem=24 * MIB):
    shapes = [jax.ShapeDtypeStruct(shape, jnp.bfloat16) for shape in outs]
    spaces = [pltpu.SMEM] * n_smem + [pltpu.VMEM] * (len(args) - n_smem)
    return pl.pallas_call(
        kernel,
        out_shape=shapes,
        in_specs=[pl.BlockSpec(memory_space=space) for space in spaces],
        out_specs=[pl.BlockSpec(memory_space=pltpu.VMEM)] * len(outs),
        compiler_params=pltpu.CompilerParams(vmem_limit_bytes=vmem),
    )(*args)


def from_group(blocks):
    return [
        blocks[0],
        lax.ppermute(blocks[1], "xl", SWAP),
        lax.ppermute(blocks[2], "zl", SWAP),
        lax.ppermute(blocks[3], ("zl", "xl"), BOTH),
    ]


def flipped(x, bits, n):
    return lax.ppermute(x, "y", [(i, i ^ bits) for i in range(n)])


def local(inputs, value_grad, value_weight, counts, offsets):
    rows, features = inputs.shape
    columns = value_grad.shape[1]
    quarter, own_columns = value_weight.shape
    n_tp, n_y, n_zh = (lax.axis_size(a) for a in (TP, "y", "zh"))
    wide = features // 4
    narrow = quarter // 4

    place = jnp.stack([lax.axis_index(a) for a in (("zl", "xl"), TP, "c", "y")]).astype(jnp.int32)
    args = (place, counts, offsets, value_grad, inputs)
    sizes = [(rows, wide + columns)] + [(rows // 2, wide + 2 * columns)] * 3
    blocks = call(prep_kernel, sizes, 3, *args, vmem=60 * MIB)
    blocks, value_weight = lax.optimization_barrier((blocks, value_weight))
    received = from_group(blocks)

    mine = value_weight.T.reshape(own_columns, 2, 2, narrow).transpose(2, 1, 0, 3)
    mine = jnp.broadcast_to(mine[:, None], (2, n_zh, 2, own_columns, narrow))
    mine = mine.reshape(-1, own_columns, narrow)
    block = lax.all_to_all(mine, ("xl", "zh", "zl"), 0, 0, tiled=True)
    received, block = lax.optimization_barrier((received, block))
    near = block.reshape(-1, narrow)
    first = flipped(near, 4, n_y)

    sizes = [(3 * rows // 2, wide), (4 * rows, columns)]
    half, own = call(split_kernel, sizes, 1, place, *received)
    half = lax.ppermute(half, "c", SWAP)
    from_far = lax.ppermute(own, "xh", SWAP)
    from_core = lax.ppermute(own, "c", SWAP)
    half, first = lax.optimization_barrier((half, first))
    (term,) = call(weight_kernel, [(n_y, wide // n_y, columns)], 0, *received, half)
    terms = lax.all_to_all(term, "y", 0, 0, tiled=True)
    near = jnp.concatenate([near, first])
    near = jnp.concatenate([near, flipped(near, 2, n_y)])
    last = flipped(near, 1, n_y)
    terms, last = lax.optimization_barrier((terms, last))
    gathered = [own, from_core, from_far, lax.ppermute(from_far, "c", SWAP)]

    sizes = (2 * n_zh, n_y, own_columns)
    kernel = functools.partial(order_kernel, sizes)
    (ordered,) = call(kernel, [(4 * rows, n_tp * columns)], 1, place, *gathered)
    outs = call(input_kernel, [(rows, narrow)] * 4, 0, ordered, near, last)

    summed = jnp.sum(terms.astype(jnp.float32), axis=0).reshape(n_zh, -1, columns)
    summed = lax.all_to_all(summed, "zh", 0, 0, tiled=True)
    normalizer = 1.0 / math.sqrt(counts.shape[1] * lax.axis_size(FSDP))
    weight_grad = jnp.sum(summed, axis=0) * normalizer

    (input_grad,) = call(join_kernel, [(rows, quarter)], 1, place, *from_group(outs))
    return (input_grad, weight_grad)


def solution(mesh):
    split = Mesh(mesh.devices.reshape(8, 2, 2, 8, 2, 2), (*FSDP, *TP))
    in_specs = (P(FSDP, None), P(FSDP, TP), P(TP, FSDP), P(FSDP, None), P(FSDP, None))
    out_specs = (P(FSDP, TP), P(FSDP, TP))
    return jax.shard_map(local, mesh=split, in_specs=in_specs, out_specs=out_specs, check_vma=False)
```

```python
import functools
import math

import jax
import jax.numpy as jnp
from jax import lax
from jax.experimental import pallas as pl
from jax.experimental.pallas import tpu as pltpu
from jax.sharding import Mesh
from jax.sharding import PartitionSpec as P

FSDP = ("zh", "zl", "xl", "y")
TP = ("xh", "c")
SWAP = [(0, 1), (1, 0)]
BOTH = [(i, i ^ 3) for i in range(4)]
MIB = 1024 * 1024


def prep_kernel(place_ref, counts_ref, offsets_ref, grad_ref, inputs_ref, own_ref, *outs):
    q, core = place_ref[0], place_ref[2]
    rows, columns = grad_ref.shape
    wide = own_ref.shape[1] - columns
    short = rows // 2
    positions = lax.broadcasted_iota(jnp.int32, (rows, columns), 0)
    length = jnp.zeros((rows, columns), jnp.int32)
    for s in range(counts_ref.shape[1]):
        first = offsets_ref[0, s]
        count = counts_ref[0, s]
        length = jnp.where((positions >= first) & (positions < first + count), count, length)
    factor = jnp.where(length > 0, lax.rsqrt(jnp.maximum(length, 1).astype(jnp.float32)), 0.0)
    scaled = (grad_ref[...].astype(jnp.float32) * factor).astype(jnp.bfloat16)
    own_ref[:, wide:] = scaled
    mine = pl.ds(pl.multiple_of(core * short, short), short)
    other = pl.ds(pl.multiple_of((1 - core) * short, short), short)
    for b in range(wide // 128):
        source = pl.ds(pl.multiple_of((4 * b + q) * 128, 128), 128)
        own_ref[:, b * 128 : (b + 1) * 128] = inputs_ref[:, source]
    for m, out_ref in enumerate(outs, 1):
        for b in range(wide // 128):
            source = pl.ds(pl.multiple_of((4 * b + (q ^ m)) * 128, 128), 128)
            out_ref[:, b * 128 : (b + 1) * 128] = inputs_ref[mine, source]
        out_ref[:, wide : wide + columns] = own_ref[mine, wide:]
        out_ref[:, wide + columns :] = own_ref[other, wide:]


def split_kernel(place_ref, own_ref, *refs):
    parts, half_ref, scaled_ref = refs[:3], refs[3], refs[4]
    core = place_ref[2]
    short, wide = parts[0].shape[0], half_ref.shape[1]
    columns = scaled_ref.shape[1]
    scaled_ref[: 2 * short, :] = own_ref[:, wide:]
    for m, part in enumerate(parts, 1):
        half_ref[(m - 1) * short : m * short, :] = part[:, :wide]
        mine = pl.ds(pl.multiple_of((2 * m + core) * short, short), short)
        other = pl.ds(pl.multiple_of((2 * m + 1 - core) * short, short), short)
        scaled_ref[mine, :] = part[:, wide : wide + columns]
        scaled_ref[other, :] = part[:, wide + columns :]


def weight_kernel(own_ref, *refs):
    parts, half_ref, out_ref = refs[:3], refs[3], refs[4]
    peers, _, columns = out_ref.shape
    wide = half_ref.shape[1]
    short = parts[0].shape[0]
    each = 128 // peers

    def product(left, right):
        dims = (((0,), (0,)), ((), ()))
        return lax.dot_general(left, right, dims, preferred_element_type=jnp.float32)

    for b in range(wide // 128):
        block = slice(b * 128, (b + 1) * 128)
        term = product(own_ref[:, block], own_ref[:, wide:])
        for m, part in enumerate(parts):
            term += product(part[:, block], part[:, wide : wide + columns])
            term += product(half_ref[m * short : (m + 1) * short, block], part[:, wide + columns :])
        out_ref[:, b * each : (b + 1) * each, :] = term.reshape(peers, each, -1).astype(jnp.bfloat16)


def order_kernel(sizes, place_ref, own_ref, core_ref, far_ref, both_ref, out_ref):
    tensor = place_ref[1]
    parts = [own_ref, core_ref, far_ref, both_ref]
    wide = own_ref.shape[1]
    n_z, n_y, n_j = sizes
    total = len(parts) * wide
    spot = lax.broadcasted_iota(jnp.int32, (1, total), 1)
    j = spot % n_j
    low = spot // n_j % 2
    z = spot // (n_j * 2) % n_z
    xl = spot // (n_j * 2 * n_z) % 2
    y = place_ref[3] ^ (spot // (n_j * 4 * n_z) * 2 + low)
    source = ((z * 2 + xl) * n_y + y) * n_j + j
    for c in range(0, total, 256):
        moved = None
        for p, part in enumerate(parts):
            row = lax.broadcasted_iota(jnp.int32, (wide, 256), 0) + (tensor ^ p) * wide
            pick = (row == source[:, c : c + 256]).astype(jnp.float32).astype(jnp.bfloat16)
            term = jnp.dot(part[...], pick, preferred_element_type=jnp.float32)
            moved = term if moved is None else moved + term
        out_ref[:, c : c + 256] = moved.astype(jnp.bfloat16)


def input_kernel(scaled_ref, *refs):
    weights, outs = refs[:-4], refs[-4:]
    rows, deep = outs[0].shape[0], weights[0].shape[0]
    for m, out_ref in enumerate(outs):
        total = None
        for f, weight in enumerate(weights):
            block = scaled_ref[m * rows : (m + 1) * rows, f * deep : (f + 1) * deep]
            term = jnp.dot(block, weight[...], preferred_element_type=jnp.float32)
            total = term if total is None else total + term
        out_ref[...] = total.astype(jnp.bfloat16)


def join_kernel(place_ref, *refs):
    parts, out_ref = refs[:4], refs[4]
    wide = parts[0].shape[1]
    for m, part in enumerate(parts):
        place = pl.multiple_of((place_ref[0] ^ m) * wide, 128)
        out_ref[:, pl.ds(place, wide)] = part[...]


def call(kernel, outs, n_smem, *args, vmem=24 * MIB):
    shapes = [jax.ShapeDtypeStruct(shape, jnp.bfloat16) for shape in outs]
    spaces = [pltpu.SMEM] * n_smem + [pltpu.VMEM] * (len(args) - n_smem)
    return pl.pallas_call(
        kernel,
        out_shape=shapes,
        in_specs=[pl.BlockSpec(memory_space=space) for space in spaces],
        out_specs=[pl.BlockSpec(memory_space=pltpu.VMEM)] * len(outs),
        compiler_params=pltpu.CompilerParams(vmem_limit_bytes=vmem),
    )(*args)


def from_group(blocks):
    return [
        blocks[0],
        lax.ppermute(blocks[1], "xl", SWAP),
        lax.ppermute(blocks[2], "zl", SWAP),
        lax.ppermute(blocks[3], ("zl", "xl"), BOTH),
    ]


def flipped(x, bits, n):
    return lax.ppermute(x, "y", [(i, i ^ bits) for i in range(n)])


def local(inputs, value_grad, value_weight, counts, offsets):
    rows, features = inputs.shape
    columns = value_grad.shape[1]
    quarter, own_columns = value_weight.shape
    n_tp, n_y, n_zh = (lax.axis_size(a) for a in (TP, "y", "zh"))
    wide = features // 4
    narrow = quarter // 4

    place = jnp.stack([lax.axis_index(a) for a in (("zl", "xl"), TP, "c", "y")]).astype(jnp.int32)
    args = (place, counts, offsets, value_grad, inputs)
    sizes = [(rows, wide + columns)] + [(rows // 2, wide + 2 * columns)] * 3
    blocks = call(prep_kernel, sizes, 3, *args, vmem=60 * MIB)
    turned = value_weight.T
    pair = jnp.concatenate([turned, flipped(turned, 1, n_y)])
    received = from_group(blocks)
    received[1], pair = lax.optimization_barrier((received[1], pair))

    mine = pair.reshape(2 * own_columns, 2, 2, narrow).transpose(2, 1, 0, 3)
    mine = jnp.broadcast_to(mine[:, None], (2, n_zh, 2, 2 * own_columns, narrow))
    mine = mine.reshape(-1, 2 * own_columns, narrow)
    block = lax.all_to_all(mine, ("xl", "zh", "zl"), 0, 0, tiled=True)
    block = block.reshape(-1, narrow)

    sizes = [(3 * rows // 2, wide), (4 * rows, columns)]
    half, own = call(split_kernel, sizes, 1, place, *received)
    half = lax.ppermute(half, "c", SWAP)
    from_far = lax.ppermute(own, "xh", SWAP)
    from_core = lax.ppermute(own, "c", SWAP)
    (term,) = call(weight_kernel, [(n_y, wide // n_y, columns)], 0, *received, half)
    terms = lax.all_to_all(term, "y", 0, 0, tiled=True)
    weights = [block] + [flipped(block, bits, n_y) for bits in range(2, n_y, 2)]
    terms, weights, from_far = lax.optimization_barrier((terms, weights, from_far))
    gathered = [own, from_core, from_far, lax.ppermute(from_far, "c", SWAP)]

    sizes = (2 * n_zh, n_y, own_columns)
    kernel = functools.partial(order_kernel, sizes)
    (ordered,) = call(kernel, [(4 * rows, n_tp * columns)], 1, place, *gathered)
    outs = call(input_kernel, [(rows, narrow)] * 4, 0, ordered, *weights)

    summed = jnp.sum(terms.astype(jnp.float32), axis=0).reshape(n_zh, -1, columns)
    summed = lax.all_to_all(summed, "zh", 0, 0, tiled=True)
    outs = from_group(outs)
    summed, outs = lax.optimization_barrier((summed, outs))
    normalizer = 1.0 / math.sqrt(counts.shape[1] * lax.axis_size(FSDP))
    weight_grad = jnp.sum(summed, axis=0) * normalizer

    (input_grad,) = call(join_kernel, [(rows, quarter)], 1, place, *outs)
    return (input_grad, weight_grad)


def solution(mesh):
    split = Mesh(mesh.devices.reshape(8, 2, 2, 8, 2, 2), (*FSDP, *TP))
    in_specs = (P(FSDP, None), P(FSDP, TP), P(TP, FSDP), P(FSDP, None), P(FSDP, None))
    out_specs = (P(FSDP, TP), P(FSDP, TP))
    return jax.shard_map(local, mesh=split, in_specs=in_specs, out_specs=out_specs, check_vma=False)
```

```python
import functools
import math

import jax
import jax.numpy as jnp
from jax import lax
from jax.experimental import pallas as pl
from jax.experimental.pallas import tpu as pltpu
from jax.sharding import Mesh
from jax.sharding import PartitionSpec as P

FSDP = ("zh", "zl", "xl", "y")
TP = ("xh", "c")
SWAP = [(0, 1), (1, 0)]
BOTH = [(i, i ^ 3) for i in range(4)]
MIB = 1024 * 1024


def prep_kernel(place_ref, counts_ref, offsets_ref, grad_ref, inputs_ref, own_ref, *outs):
    q, core = place_ref[0], place_ref[2]
    rows, columns = grad_ref.shape
    wide = own_ref.shape[1] - columns
    short = rows // 2
    positions = lax.broadcasted_iota(jnp.int32, (rows, columns), 0)
    length = jnp.zeros((rows, columns), jnp.int32)
    for s in range(counts_ref.shape[1]):
        first = offsets_ref[0, s]
        count = counts_ref[0, s]
        length = jnp.where((positions >= first) & (positions < first + count), count, length)
    factor = jnp.where(length > 0, lax.rsqrt(jnp.maximum(length, 1).astype(jnp.float32)), 0.0)
    scaled = (grad_ref[...].astype(jnp.float32) * factor).astype(jnp.bfloat16)
    own_ref[:, wide:] = scaled
    mine = pl.ds(pl.multiple_of(core * short, short), short)
    other = pl.ds(pl.multiple_of((1 - core) * short, short), short)
    for b in range(wide // 128):
        source = pl.ds(pl.multiple_of((4 * b + q) * 128, 128), 128)
        own_ref[:, b * 128 : (b + 1) * 128] = inputs_ref[:, source]
    for m, out_ref in enumerate(outs, 1):
        for b in range(wide // 128):
            source = pl.ds(pl.multiple_of((4 * b + (q ^ m)) * 128, 128), 128)
            out_ref[:, b * 128 : (b + 1) * 128] = inputs_ref[mine, source]
        out_ref[:, wide : wide + columns] = own_ref[mine, wide:]
        out_ref[:, wide + columns :] = own_ref[other, wide:]


def split_kernel(place_ref, own_ref, *refs):
    parts, half_ref, scaled_ref = refs[:3], refs[3], refs[4]
    core = place_ref[2]
    short, wide = parts[0].shape[0], half_ref.shape[1]
    columns = scaled_ref.shape[1]
    scaled_ref[: 2 * short, :] = own_ref[:, wide:]
    for m, part in enumerate(parts, 1):
        half_ref[(m - 1) * short : m * short, :] = part[:, :wide]
        mine = pl.ds(pl.multiple_of((2 * m + core) * short, short), short)
        other = pl.ds(pl.multiple_of((2 * m + 1 - core) * short, short), short)
        scaled_ref[mine, :] = part[:, wide : wide + columns]
        scaled_ref[other, :] = part[:, wide + columns :]


def weight_kernel(own_ref, *refs):
    parts, half_ref, out_ref = refs[:3], refs[3], refs[4]
    peers, _, columns = out_ref.shape
    wide = half_ref.shape[1]
    short = parts[0].shape[0]
    each = 128 // peers

    def product(left, right):
        dims = (((0,), (0,)), ((), ()))
        return lax.dot_general(left, right, dims, preferred_element_type=jnp.float32)

    for b in range(wide // 128):
        block = slice(b * 128, (b + 1) * 128)
        term = product(own_ref[:, block], own_ref[:, wide:])
        for m, part in enumerate(parts):
            term += product(part[:, block], part[:, wide : wide + columns])
            term += product(half_ref[m * short : (m + 1) * short, block], part[:, wide + columns :])
        out_ref[:, b * each : (b + 1) * each, :] = term.reshape(peers, each, -1).astype(jnp.bfloat16)


def order_kernel(sizes, place_ref, own_ref, core_ref, far_ref, both_ref, out_ref):
    q, tensor, y, zh = (place_ref[i] for i in (0, 1, 3, 4))
    parts = [own_ref, core_ref, far_ref, both_ref]
    wide = own_ref.shape[1]
    n_y, n_j = sizes
    total = len(parts) * wide
    spot = lax.broadcasted_iota(jnp.int32, (1, total), 1)
    j = spot % n_j
    y_low = spot // n_j % 2
    group = q ^ (spot // (2 * n_j) % 4)
    zh_high = spot // (8 * n_j) % 4
    zh_low = spot // (32 * n_j) % 2
    y_high = spot // (64 * n_j)
    fsdp = ((zh ^ (2 * zh_high + zh_low)) * 4 + group) * n_y + (y ^ (2 * y_high + y_low))
    source = fsdp * n_j + j
    for c in range(0, total, 256):
        moved = None
        for p, part in enumerate(parts):
            row = lax.broadcasted_iota(jnp.int32, (wide, 256), 0) + (tensor ^ p) * wide
            pick = (row == source[:, c : c + 256]).astype(jnp.float32).astype(jnp.bfloat16)
            term = jnp.dot(part[...], pick, preferred_element_type=jnp.float32)
            moved = term if moved is None else moved + term
        out_ref[:, c : c + 256] = moved.astype(jnp.bfloat16)


def input_kernel(scaled_ref, *refs):
    weights, outs = refs[:-4], refs[-4:]
    rows, deep = outs[0].shape[0], weights[0].shape[0]
    for m, out_ref in enumerate(outs):
        total = None
        for f, weight in enumerate(weights):
            block = scaled_ref[m * rows : (m + 1) * rows, f * deep : (f + 1) * deep]
            term = jnp.dot(block, weight[...], preferred_element_type=jnp.float32)
            total = term if total is None else total + term
        out_ref[...] = total.astype(jnp.bfloat16)


def join_kernel(place_ref, *refs):
    parts, out_ref = refs[:4], refs[4]
    wide = parts[0].shape[1]
    for m, part in enumerate(parts):
        place = pl.multiple_of((place_ref[0] ^ m) * wide, 128)
        out_ref[:, pl.ds(place, wide)] = part[...]


def call(kernel, outs, n_smem, *args, vmem=24 * MIB):
    shapes = [jax.ShapeDtypeStruct(shape, jnp.bfloat16) for shape in outs]
    spaces = [pltpu.SMEM] * n_smem + [pltpu.VMEM] * (len(args) - n_smem)
    return pl.pallas_call(
        kernel,
        out_shape=shapes,
        in_specs=[pl.BlockSpec(memory_space=space) for space in spaces],
        out_specs=[pl.BlockSpec(memory_space=pltpu.VMEM)] * len(outs),
        compiler_params=pltpu.CompilerParams(vmem_limit_bytes=vmem),
    )(*args)


def from_group(blocks):
    return [
        blocks[0],
        lax.ppermute(blocks[1], "xl", SWAP),
        lax.ppermute(blocks[2], "zl", SWAP),
        lax.ppermute(blocks[3], ("zl", "xl"), BOTH),
    ]


def flipped(x, axis, bits):
    return lax.ppermute(x, axis, [(i, i ^ bits) for i in range(lax.axis_size(axis))])


def local(inputs, value_grad, value_weight, counts, offsets):
    rows, features = inputs.shape
    columns = value_grad.shape[1]
    quarter, own_columns = value_weight.shape
    n_tp, n_y, n_zh = (lax.axis_size(a) for a in (TP, "y", "zh"))
    wide = features // 4
    narrow = quarter // 4

    place = jnp.stack([lax.axis_index(a) for a in (("zl", "xl"), TP, "c", "y", "zh")]).astype(jnp.int32)
    args = (place, counts, offsets, value_grad, inputs)
    sizes = [(rows, wide + columns)] + [(rows // 2, wide + 2 * columns)] * 3
    blocks = call(prep_kernel, sizes, 3, *args, vmem=60 * MIB)
    turned = value_weight.T
    pair = jnp.concatenate([turned, flipped(turned, "y", 1)])
    blocks, pair = lax.optimization_barrier((blocks, pair))
    received = from_group(blocks)
    starts = [(place[0] ^ m) * narrow for m in range(4)]
    quarters = [lax.dynamic_slice_in_dim(pair, start, narrow, 1) for start in starts]
    received, quarters = lax.optimization_barrier((received, from_group(quarters)))
    block = jnp.concatenate(quarters)
    far_z = [flipped(block, "zh", bits) for bits in (2, 4, 6)]

    sizes = [(3 * rows // 2, wide), (4 * rows, columns)]
    half, own = call(split_kernel, sizes, 1, place, *received)
    half = lax.ppermute(half, "c", SWAP)
    from_far = lax.ppermute(own, "xh", SWAP)
    from_core = lax.ppermute(own, "c", SWAP)
    half, far_z = lax.optimization_barrier((half, far_z))
    (term,) = call(weight_kernel, [(n_y, wide // n_y, columns)], 0, *received, half)
    terms = lax.all_to_all(term, "y", 0, 0, tiled=True)
    block = jnp.concatenate([block] + far_z)
    block = jnp.concatenate([block, flipped(block, "zh", 1)])
    weights = [block] + [flipped(block, "y", bits) for bits in (2, 4, 6)]
    terms, weights, from_far = lax.optimization_barrier((terms, weights, from_far))
    gathered = [own, from_core, from_far, lax.ppermute(from_far, "c", SWAP)]

    sizes = (n_y, own_columns)
    kernel = functools.partial(order_kernel, sizes)
    (ordered,) = call(kernel, [(4 * rows, n_tp * columns)], 1, place, *gathered)
    outs = call(input_kernel, [(rows, narrow)] * 4, 0, ordered, *weights)

    summed = jnp.sum(terms.astype(jnp.float32), axis=0).reshape(n_zh, -1, columns)
    summed = lax.all_to_all(summed, "zh", 0, 0, tiled=True)
    outs = from_group(outs)
    summed, outs = lax.optimization_barrier((summed, outs))
    normalizer = 1.0 / math.sqrt(counts.shape[1] * lax.axis_size(FSDP))
    weight_grad = jnp.sum(summed, axis=0) * normalizer

    (input_grad,) = call(join_kernel, [(rows, quarter)], 1, place, *outs)
    return (input_grad, weight_grad)


def solution(mesh):
    split = Mesh(mesh.devices.reshape(8, 2, 2, 8, 2, 2), (*FSDP, *TP))
    in_specs = (P(FSDP, None), P(FSDP, TP), P(TP, FSDP), P(FSDP, None), P(FSDP, None))
    out_specs = (P(FSDP, TP), P(FSDP, TP))
    return jax.shard_map(local, mesh=split, in_specs=in_specs, out_specs=out_specs, check_vma=False)
```

```python
import functools
import math

import jax
import jax.numpy as jnp
from jax import lax
from jax.experimental import pallas as pl
from jax.experimental.pallas import tpu as pltpu
from jax.sharding import Mesh
from jax.sharding import PartitionSpec as P

FSDP = ("zh", "zl", "xl", "y")
TP = ("xh", "c")
SWAP = [(0, 1), (1, 0)]
BOTH = [(i, i ^ 3) for i in range(4)]
MIB = 1024 * 1024


def prep_kernel(place_ref, counts_ref, offsets_ref, grad_ref, inputs_ref, own_ref, *outs):
    q, core = place_ref[0], place_ref[2]
    rows, columns = grad_ref.shape
    wide = own_ref.shape[1] - columns
    short = rows // 2
    positions = lax.broadcasted_iota(jnp.int32, (rows, columns), 0)
    length = jnp.zeros((rows, columns), jnp.int32)
    for s in range(counts_ref.shape[1]):
        first = offsets_ref[0, s]
        count = counts_ref[0, s]
        length = jnp.where((positions >= first) & (positions < first + count), count, length)
    factor = jnp.where(length > 0, lax.rsqrt(jnp.maximum(length, 1).astype(jnp.float32)), 0.0)
    scaled = (grad_ref[...].astype(jnp.float32) * factor).astype(jnp.bfloat16)
    own_ref[:, wide:] = scaled
    mine = pl.ds(pl.multiple_of(core * short, short), short)
    other = pl.ds(pl.multiple_of((1 - core) * short, short), short)
    for b in range(wide // 128):
        source = pl.ds(pl.multiple_of((4 * b + q) * 128, 128), 128)
        own_ref[:, b * 128 : (b + 1) * 128] = inputs_ref[:, source]
    for m, out_ref in enumerate(outs, 1):
        for b in range(wide // 128):
            source = pl.ds(pl.multiple_of((4 * b + (q ^ m)) * 128, 128), 128)
            out_ref[:, b * 128 : (b + 1) * 128] = inputs_ref[mine, source]
        out_ref[:, wide : wide + columns] = own_ref[mine, wide:]
        out_ref[:, wide + columns :] = own_ref[other, wide:]


def split_kernel(place_ref, own_ref, *refs):
    parts, half_ref, scaled_ref = refs[:3], refs[3], refs[4]
    core = place_ref[2]
    short, wide = parts[0].shape[0], half_ref.shape[1]
    columns = scaled_ref.shape[1]
    scaled_ref[: 2 * short, :] = own_ref[:, wide:]
    for m, part in enumerate(parts, 1):
        half_ref[(m - 1) * short : m * short, :] = part[:, :wide]
        mine = pl.ds(pl.multiple_of((2 * m + core) * short, short), short)
        other = pl.ds(pl.multiple_of((2 * m + 1 - core) * short, short), short)
        scaled_ref[mine, :] = part[:, wide : wide + columns]
        scaled_ref[other, :] = part[:, wide + columns :]


def weight_kernel(own_ref, *refs):
    parts, half_ref, out_ref = refs[:3], refs[3], refs[4]
    peers, _, columns = out_ref.shape
    wide = half_ref.shape[1]
    short = parts[0].shape[0]
    each = 128 // peers

    def product(left, right):
        dims = (((0,), (0,)), ((), ()))
        return lax.dot_general(left, right, dims, preferred_element_type=jnp.float32)

    for b in range(wide // 128):
        block = slice(b * 128, (b + 1) * 128)
        term = product(own_ref[:, block], own_ref[:, wide:])
        for m, part in enumerate(parts):
            term += product(part[:, block], part[:, wide : wide + columns])
            term += product(half_ref[m * short : (m + 1) * short, block], part[:, wide + columns :])
        out_ref[:, b * each : (b + 1) * each, :] = term.reshape(peers, each, -1).astype(jnp.bfloat16)


def order_kernel(sizes, place_ref, own_ref, core_ref, far_ref, both_ref, out_ref):
    tensor = place_ref[1]
    parts = [own_ref, core_ref, far_ref, both_ref]
    wide = own_ref.shape[1]
    n_z, n_y, n_j = sizes
    total = len(parts) * wide
    spot = lax.broadcasted_iota(jnp.int32, (1, total), 1)
    j = spot % n_j
    low = spot // n_j % 2
    z = spot // (n_j * 2) % n_z
    xl = spot // (n_j * 2 * n_z) % 2
    y = place_ref[3] ^ (spot // (n_j * 4 * n_z) * 2 + low)
    source = ((z * 2 + xl) * n_y + y) * n_j + j
    for c in range(0, total, 256):
        moved = None
        for p, part in enumerate(parts):
            row = lax.broadcasted_iota(jnp.int32, (wide, 256), 0) + (tensor ^ p) * wide
            pick = (row == source[:, c : c + 256]).astype(jnp.float32).astype(jnp.bfloat16)
            term = jnp.dot(part[...], pick, preferred_element_type=jnp.float32)
            moved = term if moved is None else moved + term
        out_ref[:, c : c + 256] = moved.astype(jnp.bfloat16)


def input_kernel(scaled_ref, *refs):
    weights, outs = refs[:-4], refs[-4:]
    rows, deep = outs[0].shape[0], weights[0].shape[0]
    for m, out_ref in enumerate(outs):
        total = None
        for f, weight in enumerate(weights):
            block = scaled_ref[m * rows : (m + 1) * rows, f * deep : (f + 1) * deep]
            term = jnp.dot(block, weight[...], preferred_element_type=jnp.float32)
            total = term if total is None else total + term
        out_ref[...] = total.astype(jnp.bfloat16)


def join_kernel(place_ref, *refs):
    parts, out_ref = refs[:4], refs[4]
    wide = parts[0].shape[1]
    for m, part in enumerate(parts):
        place = pl.multiple_of((place_ref[0] ^ m) * wide, 128)
        out_ref[:, pl.ds(place, wide)] = part[...]


def call(kernel, outs, n_smem, *args, vmem=24 * MIB):
    shapes = [jax.ShapeDtypeStruct(shape, jnp.bfloat16) for shape in outs]
    spaces = [pltpu.SMEM] * n_smem + [pltpu.VMEM] * (len(args) - n_smem)
    return pl.pallas_call(
        kernel,
        out_shape=shapes,
        in_specs=[pl.BlockSpec(memory_space=space) for space in spaces],
        out_specs=[pl.BlockSpec(memory_space=pltpu.VMEM)] * len(outs),
        compiler_params=pltpu.CompilerParams(vmem_limit_bytes=vmem),
    )(*args)


def from_group(blocks):
    return [
        blocks[0],
        lax.ppermute(blocks[1], "xl", SWAP),
        lax.ppermute(blocks[2], "zl", SWAP),
        lax.ppermute(blocks[3], ("zl", "xl"), BOTH),
    ]


def flipped(x, bits, n):
    return lax.ppermute(x, "y", [(i, i ^ bits) for i in range(n)])


def local(inputs, value_grad, value_weight, counts, offsets):
    rows, features = inputs.shape
    columns = value_grad.shape[1]
    quarter, own_columns = value_weight.shape
    n_tp, n_y, n_zh = (lax.axis_size(a) for a in (TP, "y", "zh"))
    wide = features // 4
    narrow = quarter // 4

    place = jnp.stack([lax.axis_index(a) for a in (("zl", "xl"), TP, "c", "y")]).astype(jnp.int32)
    args = (place, counts, offsets, value_grad, inputs)
    sizes = [(rows, wide + columns)] + [(rows // 2, wide + 2 * columns)] * 3
    blocks = call(prep_kernel, sizes, 3, *args, vmem=60 * MIB)
    turned = value_weight.T
    pair = jnp.concatenate([turned, flipped(turned, 1, n_y)])
    blocks, pair = lax.optimization_barrier((blocks, pair))
    received = from_group(blocks)

    mine = pair.reshape(2 * own_columns, 2, 2, narrow).transpose(2, 1, 0, 3)
    mine = jnp.broadcast_to(mine[:, None], (2, n_zh, 2, 2 * own_columns, narrow))
    mine = mine.reshape(-1, 2 * own_columns, narrow)
    block = lax.all_to_all(mine, ("xl", "zh", "zl"), 0, 0, tiled=True)
    received, block = lax.optimization_barrier((received, block))
    block = block.reshape(-1, narrow)

    sizes = [(3 * rows // 2, wide), (4 * rows, columns)]
    half, own = call(split_kernel, sizes, 1, place, *received)
    half = lax.ppermute(half, "c", SWAP)
    from_far = lax.ppermute(own, "xh", SWAP)
    from_core = lax.ppermute(own, "c", SWAP)
    (term,) = call(weight_kernel, [(n_y, wide // n_y, columns)], 0, *received, half)
    terms = lax.all_to_all(term, "y", 0, 0, tiled=True)
    weights = [block] + [flipped(block, bits, n_y) for bits in range(2, n_y, 2)]
    terms, weights, from_far = lax.optimization_barrier((terms, weights, from_far))
    gathered = [own, from_core, from_far, lax.ppermute(from_far, "c", SWAP)]

    sizes = (2 * n_zh, n_y, own_columns)
    kernel = functools.partial(order_kernel, sizes)
    (ordered,) = call(kernel, [(4 * rows, n_tp * columns)], 1, place, *gathered)
    outs = call(input_kernel, [(rows, narrow)] * 4, 0, ordered, *weights)

    summed = jnp.sum(terms.astype(jnp.float32), axis=0).reshape(n_zh, -1, columns)
    summed = lax.all_to_all(summed, "zh", 0, 0, tiled=True)
    outs = from_group(outs)
    summed, outs = lax.optimization_barrier((summed, outs))
    normalizer = 1.0 / math.sqrt(counts.shape[1] * lax.axis_size(FSDP))
    weight_grad = jnp.sum(summed, axis=0) * normalizer

    (input_grad,) = call(join_kernel, [(rows, quarter)], 1, place, *outs)
    return (input_grad, weight_grad)


def solution(mesh):
    split = Mesh(mesh.devices.reshape(8, 2, 2, 8, 2, 2), (*FSDP, *TP))
    in_specs = (P(FSDP, None), P(FSDP, TP), P(TP, FSDP), P(FSDP, None), P(FSDP, None))
    out_specs = (P(FSDP, TP), P(FSDP, TP))
    return jax.shard_map(local, mesh=split, in_specs=in_specs, out_specs=out_specs, check_vma=False)
```

```python
import functools
import math

import jax
import jax.numpy as jnp
from jax import lax
from jax.experimental import pallas as pl
from jax.experimental.pallas import tpu as pltpu
from jax.sharding import Mesh
from jax.sharding import PartitionSpec as P

FSDP = ("zh", "zl", "xl", "y")
TP = ("xh", "c")
SWAP = [(0, 1), (1, 0)]
BOTH = [(i, i ^ 3) for i in range(4)]
MIB = 1024 * 1024


def prep_kernel(place_ref, counts_ref, offsets_ref, grad_ref, inputs_ref, own_ref, *outs):
    q, core = place_ref[0], place_ref[2]
    rows, columns = grad_ref.shape
    wide = own_ref.shape[1] - columns
    short = rows // 2
    positions = lax.broadcasted_iota(jnp.int32, (rows, columns), 0)
    length = jnp.zeros((rows, columns), jnp.int32)
    for s in range(counts_ref.shape[1]):
        first = offsets_ref[0, s]
        count = counts_ref[0, s]
        length = jnp.where((positions >= first) & (positions < first + count), count, length)
    factor = jnp.where(length > 0, lax.rsqrt(jnp.maximum(length, 1).astype(jnp.float32)), 0.0)
    scaled = (grad_ref[...].astype(jnp.float32) * factor).astype(jnp.bfloat16)
    own_ref[:, wide:] = scaled
    mine = pl.ds(pl.multiple_of(core * short, short), short)
    other = pl.ds(pl.multiple_of((1 - core) * short, short), short)
    for b in range(wide // 128):
        source = pl.ds(pl.multiple_of((4 * b + q) * 128, 128), 128)
        own_ref[:, b * 128 : (b + 1) * 128] = inputs_ref[:, source]
    for m, out_ref in enumerate(outs, 1):
        for b in range(wide // 128):
            source = pl.ds(pl.multiple_of((4 * b + (q ^ m)) * 128, 128), 128)
            out_ref[:, b * 128 : (b + 1) * 128] = inputs_ref[mine, source]
        out_ref[:, wide : wide + columns] = own_ref[mine, wide:]
        out_ref[:, wide + columns :] = own_ref[other, wide:]


def split_kernel(place_ref, own_ref, *refs):
    parts, half_ref, scaled_ref = refs[:3], refs[3], refs[4]
    core = place_ref[2]
    short, wide = parts[0].shape[0], half_ref.shape[1]
    columns = scaled_ref.shape[1]
    scaled_ref[: 2 * short, :] = own_ref[:, wide:]
    for m, part in enumerate(parts, 1):
        half_ref[(m - 1) * short : m * short, :] = part[:, :wide]
        mine = pl.ds(pl.multiple_of((2 * m + core) * short, short), short)
        other = pl.ds(pl.multiple_of((2 * m + 1 - core) * short, short), short)
        scaled_ref[mine, :] = part[:, wide : wide + columns]
        scaled_ref[other, :] = part[:, wide + columns :]


def weight_kernel(own_ref, *refs):
    parts, half_ref, out_ref = refs[:3], refs[3], refs[4]
    peers, _, columns = out_ref.shape
    wide = half_ref.shape[1]
    short = parts[0].shape[0]
    each = 128 // peers

    def product(left, right):
        dims = (((0,), (0,)), ((), ()))
        return lax.dot_general(left, right, dims, preferred_element_type=jnp.float32)

    for b in range(wide // 128):
        block = slice(b * 128, (b + 1) * 128)
        term = product(own_ref[:, block], own_ref[:, wide:])
        for m, part in enumerate(parts):
            term += product(part[:, block], part[:, wide : wide + columns])
            term += product(half_ref[m * short : (m + 1) * short, block], part[:, wide + columns :])
        out_ref[:, b * each : (b + 1) * each, :] = term.reshape(peers, each, -1).astype(jnp.bfloat16)


def order_kernel(sizes, place_ref, own_ref, core_ref, far_ref, both_ref, out_ref):
    tensor = place_ref[1]
    parts = [own_ref, core_ref, far_ref, both_ref]
    wide = own_ref.shape[1]
    n_z, n_y, n_j = sizes
    total = len(parts) * wide
    spot = lax.broadcasted_iota(jnp.int32, (1, total), 1)
    j = spot % n_j
    z = (spot // n_j) % n_z
    xl = (spot // (n_j * n_z)) % 2
    flip = spot // (n_j * n_z * 2)
    y = place_ref[3] ^ ((flip % 2) * 4 + (flip // 2 % 2) * 2 + flip // 4)
    source = ((z * 2 + xl) * n_y + y) * n_j + j
    for c in range(0, total, 256):
        moved = None
        for p, part in enumerate(parts):
            row = lax.broadcasted_iota(jnp.int32, (wide, 256), 0) + (tensor ^ p) * wide
            pick = (row == source[:, c : c + 256]).astype(jnp.float32).astype(jnp.bfloat16)
            term = jnp.dot(part[...], pick, preferred_element_type=jnp.float32)
            moved = term if moved is None else moved + term
        out_ref[:, c : c + 256] = moved.astype(jnp.bfloat16)


def input_kernel(scaled_ref, near_ref, next_ref, *outs):
    rows, deep = outs[0].shape[0], near_ref.shape[0]
    for m, out_ref in enumerate(outs):
        block = slice(m * rows, (m + 1) * rows)
        total = jnp.dot(
            scaled_ref[block, :deep], near_ref[...], preferred_element_type=jnp.float32
        )
        total += jnp.dot(
            scaled_ref[block, deep:], next_ref[...], preferred_element_type=jnp.float32
        )
        out_ref[...] = total.astype(jnp.bfloat16)


def join_kernel(place_ref, *refs):
    parts, out_ref = refs[:4], refs[4]
    wide = parts[0].shape[1]
    for m, part in enumerate(parts):
        place = pl.multiple_of((place_ref[0] ^ m) * wide, 128)
        out_ref[:, pl.ds(place, wide)] = part[...]


def call(kernel, outs, n_smem, *args, vmem=24 * MIB):
    shapes = [jax.ShapeDtypeStruct(shape, jnp.bfloat16) for shape in outs]
    spaces = [pltpu.SMEM] * n_smem + [pltpu.VMEM] * (len(args) - n_smem)
    return pl.pallas_call(
        kernel,
        out_shape=shapes,
        in_specs=[pl.BlockSpec(memory_space=space) for space in spaces],
        out_specs=[pl.BlockSpec(memory_space=pltpu.VMEM)] * len(outs),
        compiler_params=pltpu.CompilerParams(vmem_limit_bytes=vmem),
    )(*args)


def from_group(blocks):
    return [
        blocks[0],
        lax.ppermute(blocks[1], "xl", SWAP),
        lax.ppermute(blocks[2], "zl", SWAP),
        lax.ppermute(blocks[3], ("zl", "xl"), BOTH),
    ]


def flipped(x, bits, n):
    return lax.ppermute(x, "y", [(i, i ^ bits) for i in range(n)])


def local(inputs, value_grad, value_weight, counts, offsets):
    rows, features = inputs.shape
    columns = value_grad.shape[1]
    quarter, own_columns = value_weight.shape
    n_tp, n_y, n_zh = (lax.axis_size(a) for a in (TP, "y", "zh"))
    wide = features // 4
    narrow = quarter // 4

    place = jnp.stack([lax.axis_index(a) for a in (("zl", "xl"), TP, "c", "y")]).astype(jnp.int32)
    args = (place, counts, offsets, value_grad, inputs)
    sizes = [(rows, wide + columns)] + [(rows // 2, wide + 2 * columns)] * 3
    blocks = call(prep_kernel, sizes, 3, *args, vmem=60 * MIB)
    blocks, value_weight = lax.optimization_barrier((blocks, value_weight))
    received = from_group(blocks)

    mine = value_weight.T.reshape(own_columns, 2, 2, narrow).transpose(2, 1, 0, 3)
    mine = jnp.broadcast_to(mine[:, None], (2, n_zh, 2, own_columns, narrow))
    mine = mine.reshape(-1, own_columns, narrow)
    block = lax.all_to_all(mine, ("xl", "zh", "zl"), 0, 0, tiled=True)
    received, block = lax.optimization_barrier((received, block))
    near = block.reshape(-1, narrow)
    first = flipped(near, 4, n_y)

    sizes = [(3 * rows // 2, wide), (4 * rows, columns)]
    half, own = call(split_kernel, sizes, 1, place, *received)
    half = lax.ppermute(half, "c", SWAP)
    from_far = lax.ppermute(own, "xh", SWAP)
    from_core = lax.ppermute(own, "c", SWAP)
    half, first = lax.optimization_barrier((half, first))
    (term,) = call(weight_kernel, [(n_y, wide // n_y, columns)], 0, *received, half)
    terms = lax.all_to_all(term, "y", 0, 0, tiled=True)
    near = jnp.concatenate([near, first])
    near = jnp.concatenate([near, flipped(near, 2, n_y)])
    terms, near = lax.optimization_barrier((terms, near))
    last = flipped(near, 1, n_y)
    gathered = [own, from_core, from_far, lax.ppermute(from_far, "c", SWAP)]

    sizes = (2 * n_zh, n_y, own_columns)
    kernel = functools.partial(order_kernel, sizes)
    (ordered,) = call(kernel, [(4 * rows, n_tp * columns)], 1, place, *gathered)
    outs = call(input_kernel, [(rows, narrow)] * 4, 0, ordered, near, last)

    summed = jnp.sum(terms.astype(jnp.float32), axis=0).reshape(n_zh, -1, columns)
    summed = lax.all_to_all(summed, "zh", 0, 0, tiled=True)
    normalizer = 1.0 / math.sqrt(counts.shape[1] * lax.axis_size(FSDP))
    weight_grad = jnp.sum(summed, axis=0) * normalizer

    (input_grad,) = call(join_kernel, [(rows, quarter)], 1, place, *from_group(outs))
    return (input_grad, weight_grad)


def solution(mesh):
    split = Mesh(mesh.devices.reshape(8, 2, 2, 8, 2, 2), (*FSDP, *TP))
    in_specs = (P(FSDP, None), P(FSDP, TP), P(TP, FSDP), P(FSDP, None), P(FSDP, None))
    out_specs = (P(FSDP, TP), P(FSDP, TP))
    return jax.shard_map(local, mesh=split, in_specs=in_specs, out_specs=out_specs, check_vma=False)
```
